128 devices in a mesh: dp: 8 (over y, core), ctx: 16 (over z, x).
Axes of the slice: x: 4, y: 4, z: 4, core: 2. Of those that a mesh axis runs over, the one named last changes fastest.
Arguments:
- queries: bfloat16 [8, 2048, 8192], P('dp', 'ctx'), may hold values from -8 to 8
- key_vectors: bfloat16 [8, 2048, 8192], P('dp', 'ctx'), may hold values from -8 to 8
- value_vectors: bfloat16 [8, 2048, 8192], P('dp', 'ctx'), may hold values from -6 to 6
- out_grad: bfloat16 [8, 2048, 8192], P('dp', 'ctx'), may hold values from -6 to 6
- doc_lengths: int32 [8, 16], P('dp'), may hold values from 1 to 384, 2048 in all within a row
Outputs:
- attended: bfloat16 [8, 2048, 8192], P('dp', 'ctx')
- log_totals: float32 [8, 64, 2048], P('dp', None, 'ctx')
- query_grad: bfloat16 [8, 2048, 8192], P('dp', 'ctx')
- key_grad: bfloat16 [8, 2048, 8192], P('dp', 'ctx')
- value_grad: bfloat16 [8, 2048, 8192], P('dp', 'ctx')
The draws below stay inside these ranges and needn't reach their ends.
Inputs may be any that keep to these rules, and one draw needn't show every extreme that they name: `doc_lengths`: each row of 16 lengths sums to 2048; in every row the largest is exactly 384.
All inputs are finite; a program needn't handle non-finite values.
Results may differ from the reference program's by a relative error of at most 0.024.
Values may be sent and summed in bfloat16 or wider, within the bound.
A program may use at most 256 MiB of HBM per device.

```python
import math
import jax
import jax.numpy as jnp
import numpy as np
from jax import lax

H = 64
DH = 128
TOK_DEV = 128
SPAN = 3
SEQ = 2048
SEQS = 8
DOCS = 16
N_CTX = 16


def draw_queries(key, part):
    own_key = jax.random.fold_in(key, 1)
    return jnp.clip(jax.random.normal(own_key, (SEQS, SEQ, H * DH), jnp.float32), -6.0, 6.0).astype(jnp.bfloat16)


def draw_key_vectors(key, part):
    own_key = jax.random.fold_in(key, 2)
    return jnp.clip(jax.random.normal(own_key, (SEQS, SEQ, H * DH), jnp.float32), -6.0, 6.0).astype(jnp.bfloat16)


def block_levels(key, dims, split, smallest, largest):
    def one(dim, blocks):
        heights = jax.random.uniform(jax.random.fold_in(jax.random.fold_in(key, 6), dim), (blocks,), jnp.float32, smallest / len(split), largest / len(split))
        return jnp.repeat(jnp.exp(heights), dims[dim] // blocks).reshape((-1,) + (1,) * (len(dims) - dim - 1))

    gain = one(*split[0])
    for cut in split[1:]:
        gain = gain * one(*cut)
    return gain


def profile(count, total, limit, skew):
    portions = [(1 << 20) // math.isqrt(grade ** skew) + 1 for grade in range(2, count + 1)]
    surplus, given = total - limit - (count - 1), [1] * (count - 1)
    while surplus > 0:
        candidates = [i for i in range(count - 1) if given[i] < limit]
        mass, left = sum([portions[i] for i in candidates]), surplus
        for i in candidates:
            extra = min(limit - given[i], max(1, left * portions[i] // mass), surplus)
            given[i] = given[i] + extra
            surplus = surplus - extra
    return np.array([limit] + given)


def ragged_sizes(key, amount, total, limit, lean):
    if amount == 2:
        one = jax.random.randint(key, (), max(1, total - limit), min(limit, total - 1) + 1)
        return jnp.stack([one, total - one])
    sizes = jnp.asarray(profile(amount, total, limit, lean), jnp.int32)
    twos = (amount - 1) // 2
    source_of, sink = sizes[1:1 + 2 * twos:2], sizes[2:2 + 2 * twos:2]
    room = jnp.minimum(source_of - 1, limit - sink)
    moved = jax.random.randint(jax.random.fold_in(key, 1), (twos,), 0, 1 << 20) % (room + 1)
    sizes = sizes.at[1:1 + 2 * twos:2].set(source_of - moved).at[2:2 + 2 * twos:2].set(sink + moved)
    return sizes[jax.random.permutation(jax.random.fold_in(key, 2), amount)]


def centred(stream_key, extent, scale, limit, split=(), kind=jnp.bfloat16):
    drawn = jax.random.normal(stream_key, extent, jnp.float32) * scale
    if len(split) > 0:
        drawn = block_levels(stream_key, extent, split, -0.22, 0.18) * drawn
    return jnp.clip(drawn, min=-limit, max=limit).astype(kind)


def setup_inputs(seed: int = 0) -> dict:
    keys = jax.random.split(jax.random.key(seed), 6)
    return {
        "queries": draw_queries(jax.random.fold_in(keys[5], 71), 0),
        "key_vectors": draw_key_vectors(jax.random.fold_in(keys[5], 71), 0),
        "value_vectors": centred(keys[2], (SEQS, SEQ, H * DH), 1.0, 6.0, ((0, 8), (1, 16))),
        "out_grad": centred(keys[3], (SEQS, SEQ, H * DH), 1.0, 6.0, ((0, 8), (1, 16))),
        "doc_lengths": jax.vmap(lambda own: ragged_sizes(own, DOCS, SEQ, SPAN * TOK_DEV, 2))(jax.random.split(keys[4], SEQS)).reshape((SEQS, DOCS)).astype(jnp.int32),
    }


def first_visible(lengths, positions):
    starts = jnp.cumsum(lengths, dtype=jnp.int32) - lengths
    hit = starts[None, :] <= positions[:, None]
    return jnp.max(jnp.where(hit, starts[None, :], 0), axis=1)


def assemble(near_part, far_part):
    total = near_part
    for distance in range(1, SPAN + 1):
        piece = far_part[distance:, SPAN - distance].astype(jnp.float32)
        piece = jnp.pad(piece, ((0, distance), (0, 0), (0, 0)))
        total = total + piece
    return total.reshape(SEQ, H * DH).astype(jnp.bfloat16)


def reference(queries, key_vectors, value_vectors, out_grad, doc_lengths):
    scale = DH ** -0.5
    window = (SPAN + 1) * TOK_DEV
    margin = SPAN * TOK_DEV

    def one_sequence(inputs):
        query_seq, key_seq, value_seq, grad_seq, lengths = inputs
        key_padded = jnp.pad(key_seq, ((margin, 0), (0, 0)))
        value_padded = jnp.pad(value_seq, ((margin, 0), (0, 0)))

        def one_shard(shard):
            begin = (shard * TOK_DEV).astype(jnp.int32)
            query_rows = lax.dynamic_slice_in_dim(query_seq, begin, TOK_DEV, 0).astype(jnp.float32).reshape(TOK_DEV, H, DH)
            grad_rows = lax.dynamic_slice_in_dim(grad_seq, begin, TOK_DEV, 0).astype(jnp.float32).reshape(TOK_DEV, H, DH)
            key_rows = lax.dynamic_slice_in_dim(key_padded, begin, window, 0).astype(jnp.float32).reshape(window, H, DH)
            value_rows = lax.dynamic_slice_in_dim(value_padded, begin, window, 0).astype(jnp.float32).reshape(window, H, DH)
            query_pos = begin + jnp.arange(TOK_DEV, dtype=jnp.int32)
            key_pos = begin - margin + jnp.arange(window, dtype=jnp.int32)
            first = first_visible(lengths, query_pos)
            mask = (key_pos[None, :] >= first[:, None]) & (key_pos[None, :] <= query_pos[:, None])
            scores = jnp.einsum("qhd,khd->hqk", query_rows, key_rows) * scale
            scores = jnp.where(mask[None], scores, -jnp.inf)
            peak = jnp.max(scores, axis=2, keepdims=True)
            totals = jnp.sum(jnp.exp(scores - peak), axis=2, keepdims=True)
            log_total = peak + jnp.log(totals)
            weights = jnp.exp(scores - log_total)
            weights_low = lax.optimization_barrier(weights.astype(jnp.bfloat16)).astype(jnp.float32)
            attended = jnp.einsum("hqk,khd->qhd", weights_low, value_rows).astype(jnp.bfloat16)
            attended_wide = lax.optimization_barrier(attended).astype(jnp.float32)
            along = jnp.transpose(jnp.sum(attended_wide * grad_rows, axis=2))[:, :, None]
            pulls = jnp.einsum("qhd,khd->hqk", grad_rows, value_rows)
            slopes = lax.optimization_barrier((weights * (pulls - along)).astype(jnp.bfloat16)).astype(jnp.float32)
            query_grad = (jnp.einsum("hqk,khd->qhd", slopes, key_rows) * scale).astype(jnp.bfloat16)
            key_terms = (jnp.einsum("hqk,qhd->khd", slopes, query_rows) * scale).reshape(SPAN + 1, TOK_DEV, H * DH)
            value_terms = jnp.einsum("hqk,qhd->khd", weights_low, grad_rows).reshape(SPAN + 1, TOK_DEV, H * DH)
            key_far = lax.optimization_barrier(key_terms[:SPAN].astype(jnp.bfloat16))
            value_far = lax.optimization_barrier(value_terms[:SPAN].astype(jnp.bfloat16))
            return (attended.reshape(TOK_DEV, H * DH), log_total[:, :, 0], query_grad.reshape(TOK_DEV, H * DH),
                    key_terms[SPAN], key_far, value_terms[SPAN], value_far)

        results = lax.map(one_shard, jnp.arange(N_CTX, dtype=jnp.int32))
        attended = results[0].reshape(SEQ, H * DH)
        log_totals = jnp.transpose(results[1], (1, 0, 2)).reshape(H, SEQ)
        query_grad = results[2].reshape(SEQ, H * DH)
        key_grad = assemble(results[3], results[4])
        value_grad = assemble(results[5], results[6])
        return (attended, log_totals, query_grad, key_grad, value_grad)

    outputs = lax.map(one_sequence, (queries, key_vectors, value_vectors, out_grad, doc_lengths))
    return (outputs[0], outputs[1], outputs[2], outputs[3], outputs[4])
```

```python
import functools

import jax
import jax.numpy as jnp
from jax import lax
from jax.experimental import pallas as pl
from jax.experimental.pallas import tpu as pltpu
from jax.sharding import PartitionSpec as P

DH = 128
SPAN = 3
ROWS = 128
RING = 4
WINDOW = (SPAN + 1) * ROWS
CHUNKS = 4
AHEAD = 2
LOG2E = 1.4426950408889634
LN2 = 0.6931471805599453
MASKED = -1e30
MESH = pl.DeviceIdType.MESH

NT = (((1,), (1,)), ((), ()))
NN = (((1,), (0,)), ((), ()))
TN = (((0,), (0,)), ((), ()))


def dot(a, b, dims):
    return lax.dot_general(a, b, dims, preferred_element_type=jnp.float32)


def kernel(
    group,
    lengths,
    q_in,
    k_in,
    v_in,
    g_in,
    o_out,
    lse_out,
    dq_out,
    dk_out,
    dv_out,
    qb,
    kb,
    vb,
    gb,
    ob,
    dqb,
    lseb,
    own_k,
    own_v,
    far_k,
    far_v,
    near_k,
    near_v,
    fin_k,
    fin_v,
    bias,
    in_send,
    in_recv,
    halo_send,
    halo_recv,
    back_send,
    back_recv,
    out_send,
    out_recv,
    lse_send,
    lse_recv,
    in_local,
    out_local,
    lse_local,
):
    heads = group // DH
    width = group // CHUNKS
    per_chunk = width // DH
    dp = lax.axis_index("dp")
    ctx = lax.axis_index("ctx")
    z, x = ctx // RING, ctx % RING
    rings = lax.axis_size("ctx") // RING
    ahead = (dp, ((z + 1) % rings) * RING + x)
    behind = (dp, ((z + rings - 1) % rings) * RING + x)

    def at(step):
        return (x + step) % RING

    def peer(step):
        return (dp, z * RING + at(step))

    def span(start, size):
        return pl.ds(pl.multiple_of(start, DH), size)

    steps = (2, 1, 3)
    inputs = ((k_in, kb, SPAN), (v_in, vb, SPAN), (q_in, qb, 0), (g_in, gb, 0))

    barrier = pltpu.get_barrier_semaphore()
    for device in (peer(1), peer(2), peer(3), ahead, behind):
        pl.semaphore_signal(barrier, inc=1, device_id=device, device_id_type=MESH)
    pl.semaphore_wait(barrier, 5)

    def input_copy(c, a, step, sender):
        source, buffer, first = inputs[a]
        return pltpu.make_async_remote_copy(
            source.at[0, :, span(at(step) * group + c * width, width)],
            buffer.at[first + sender, :, span(c * width, width)],
            in_send.at[c, a, step - 1],
            in_recv.at[c, a, step - 1],
            device_id=peer(step),
            device_id_type=MESH,
        )

    def send_inputs(c):
        for a in range(4):
            for step in steps:
                input_copy(c, a, step, x).start()

    def wait_inputs(c, arrays):
        for a in arrays:
            for step in steps:
                input_copy(c, a, step, at(RING - step)).wait_recv()

    def local_input(a):
        source, buffer, first = inputs[a]
        return pltpu.make_async_copy(
            source.at[0, :, span(x * group, group)], buffer.at[first + x], in_local.at[a]
        )

    def halo_copy(c, a):
        buffer = (kb, vb)[a]
        columns = span(c * width, width)
        return pltpu.make_async_remote_copy(
            buffer.at[pl.ds(RING, SPAN), :, columns],
            buffer.at[pl.ds(0, SPAN), :, columns],
            halo_send.at[c, a],
            halo_recv.at[c, a],
            device_id=ahead,
            device_id_type=MESH,
        )

    def back_copy(c, a):
        columns = span(c * width, width)
        return pltpu.make_async_remote_copy(
            (far_k, far_v)[a].at[:, :, columns],
            (near_k, near_v)[a].at[:, :, columns],
            back_send.at[c, a],
            back_recv.at[c, a],
            device_id=behind,
            device_id_type=MESH,
        )

    outputs = ((ob, o_out), (dqb, dq_out), (fin_k, dk_out), (fin_v, dv_out))

    def output_copy(c, a, step):
        staged, out = outputs[a]
        return pltpu.make_async_remote_copy(
            staged.at[at(step), :, span(c * width, width)],
            out.at[0, :, span(x * group + c * width, width)],
            out_send.at[c, a, step - 1],
            out_recv.at[c, a, step - 1],
            device_id=peer(step),
            device_id_type=MESH,
        )

    def arrived_output(c, a, step):
        staged, out = outputs[a]
        return pltpu.make_async_remote_copy(
            staged.at[at(step), :, span(c * width, width)],
            out.at[0, :, span(at(RING - step) * group + c * width, width)],
            out_send.at[c, a, step - 1],
            out_recv.at[c, a, step - 1],
            device_id=peer(step),
            device_id_type=MESH,
        )

    def local_output(c, a):
        staged, out = outputs[a]
        return pltpu.make_async_copy(
            staged.at[x, :, span(c * width, width)],
            out.at[0, :, span(x * group + c * width, width)],
            out_local.at[c, a],
        )

    def send_outputs(c, arrays):
        for a in arrays:
            for step in steps:
                output_copy(c, a, step).start()
            local_output(c, a).start()

    def lse_copy(step, sender):
        return pltpu.make_async_remote_copy(
            lseb.at[at(step)],
            lse_out.at[0, pl.ds(pl.multiple_of(sender * heads, 8), heads), :],
            lse_send.at[step - 1],
            lse_recv.at[step - 1],
            device_id=peer(step),
            device_id_type=MESH,
        )

    for c in range(AHEAD):
        send_inputs(c)
    for a in range(4):
        local_input(a).start()

    for i in range(RING):
        base = (z * RING + i) * ROWS
        query_pos = base + lax.broadcasted_iota(jnp.int32, (1, ROWS), 1)
        first = jnp.zeros((1, ROWS), jnp.int32)
        start = jnp.int32(0)
        for d in range(lengths.shape[1]):
            first = jnp.where(start <= query_pos, start, first)
            start = start + lengths[0, d]
        key_pos = base - SPAN * ROWS + lax.broadcasted_iota(jnp.int32, (WINDOW, ROWS), 0)
        bias[i] = jnp.where((key_pos >= first) & (key_pos <= query_pos), 0.0, MASKED)

    for a in range(4):
        local_input(a).wait()

    scale = DH ** (-0.5)

    def one_head(h):
        columns = span(h * DH, DH)
        weights, slopes, query_blocks, grad_blocks = [], [], [], []
        for i in range(RING):
            keys = kb[i : i + SPAN + 1, :, columns].reshape(WINDOW, DH)
            values = vb[i : i + SPAN + 1, :, columns].reshape(WINDOW, DH)
            queries = qb[i, :, columns]
            grads = gb[i, :, columns]
            scores = dot(keys, queries, NT) * (scale * LOG2E) + bias[i]
            peak = jnp.max(scores, axis=0, keepdims=True)
            powers = jnp.exp2(scores - peak)
            totals = jnp.sum(powers, axis=0, keepdims=True)
            lseb[i, pl.ds(h, 1), :] = (peak + jnp.log2(totals)) * LN2
            weight = powers * (1.0 / totals)
            weight_low = weight.astype(jnp.bfloat16)
            pulls = dot(values, grads, NT)
            weighted = weight * pulls
            along = jnp.sum(weighted, axis=0, keepdims=True)
            slope = (weighted - weight * along).astype(jnp.bfloat16)
            ob[i, :, columns] = dot(weight_low, values, TN).astype(jnp.bfloat16)
            dqb[i, :, columns] = (dot(slope, keys, TN) * scale).astype(jnp.bfloat16)
            weights.append(weight_low)
            slopes.append(slope)
            query_blocks.append(queries)
            grad_blocks.append(grads)
        for j in range(SPAN + RING):
            seen = range(max(0, j - SPAN), min(RING - 1, j) + 1)

            def gather(parts):
                return jnp.concatenate(
                    [parts[i][(j - i) * ROWS : (j - i + 1) * ROWS] for i in seen], axis=1
                )

            def stack(blocks):
                return jnp.concatenate([blocks[i] for i in seen], axis=0)

            key_part = dot(gather(slopes), stack(query_blocks), NN) * scale
            value_part = dot(gather(weights), stack(grad_blocks), NN)
            if j < SPAN:
                far_k[j, :, columns] = key_part.astype(jnp.bfloat16)
                far_v[j, :, columns] = value_part.astype(jnp.bfloat16)
            else:
                own_k[j - SPAN, :, columns] = key_part
                own_v[j - SPAN, :, columns] = value_part

    def finish(c):
        columns = span(c * width, width)
        for a, (own, near, fin) in enumerate(
            ((own_k, near_k, fin_k), (own_v, near_v, fin_v))
        ):
            back_copy(c, a).wait_recv()
            fin[0, :, columns] = own[0, :, columns].astype(jnp.bfloat16)
            for s in range(1, RING):
                total = own[s, :, columns] + near[s - 1, :, columns].astype(jnp.float32)
                fin[s, :, columns] = total.astype(jnp.bfloat16)
        send_outputs(c, (2, 3))

    def one_chunk(c, carry):
        wait_inputs(c, (0, 1))
        for a in range(2):
            halo_copy(c, a).start()

        @pl.when(c + AHEAD < CHUNKS)
        def _():
            send_inputs(c + AHEAD)

        wait_inputs(c, (2, 3))
        for a in range(2):
            halo_copy(c, a).wait_recv()

        def head_step(h, inner):
            one_head(c * per_chunk + h)
            return inner

        lax.fori_loop(0, per_chunk, head_step, 0)
        for a in range(2):
            back_copy(c, a).start()
        send_outputs(c, (0, 1))

        @pl.when(c >= 1)
        def _():
            finish(c - 1)

        return carry

    lax.fori_loop(0, CHUNKS, one_chunk, 0)
    for step in steps:
        lse_copy(step, x).start()
    own_lse = pltpu.make_async_copy(
        lseb.at[x], lse_out.at[0, pl.ds(pl.multiple_of(x * heads, 8), heads), :], lse_local.at[0]
    )
    own_lse.start()
    finish(CHUNKS - 1)

    def drain(c, carry):
        for a in range(2):
            halo_copy(c, a).wait_send()
            back_copy(c, a).wait_send()
        for a in range(4):
            local_output(c, a).wait()
            for step in steps:
                input_copy(c, a, step, x).wait_send()
                output_copy(c, a, step).wait_send()
                arrived_output(c, a, step).wait_recv()
        return carry

    lax.fori_loop(0, CHUNKS, drain, 0)
    own_lse.wait()
    for step in steps:
        lse_copy(step, x).wait_send()
        lse_copy(step, at(RING - step)).wait_recv()


def attend(queries, key_vectors, value_vectors, out_grad, lengths):
    _, rows, all_width = queries.shape
    group = all_width // RING
    heads = group // DH
    block = jax.ShapeDtypeStruct(queries.shape, jnp.bfloat16)
    totals = jax.ShapeDtypeStruct((1, all_width // DH, rows), jnp.float32)
    anywhere = pl.BlockSpec(memory_space=pl.ANY)
    low = functools.partial(pltpu.VMEM, dtype=jnp.bfloat16)
    wide = functools.partial(pltpu.VMEM, dtype=jnp.float32)
    copies = pltpu.SemaphoreType.DMA
    return pl.pallas_call(
        functools.partial(kernel, group),
        name="spread_heads_attention",
        out_shape=(block, totals, block, block, block),
        in_specs=[pl.BlockSpec(memory_space=pltpu.SMEM)] + [anywhere] * 4,
        out_specs=(anywhere,) * 5,
        scratch_shapes=[
            low((RING, rows, group)),
            low((SPAN + RING, rows, group)),
            low((SPAN + RING, rows, group)),
            low((RING, rows, group)),
            low((RING, rows, group)),
            low((RING, rows, group)),
            wide((RING, heads, rows)),
            wide((RING, rows, group)),
            wide((RING, rows, group)),
            low((SPAN, rows, group)),
            low((SPAN, rows, group)),
            low((SPAN, rows, group)),
            low((SPAN, rows, group)),
            low((RING, rows, group)),
            low((RING, rows, group)),
            wide((RING, WINDOW, ROWS)),
            copies((CHUNKS, 4, 3)),
            copies((CHUNKS, 4, 3)),
            copies((CHUNKS, 2)),
            copies((CHUNKS, 2)),
            copies((CHUNKS, 2)),
            copies((CHUNKS, 2)),
            copies((CHUNKS, 4, 3)),
            copies((CHUNKS, 4, 3)),
            copies((3,)),
            copies((3,)),
            copies((4,)),
            copies((CHUNKS, 4)),
            copies((1,)),
        ],
        compiler_params=pltpu.CompilerParams(
            collective_id=0, has_side_effects=True, vmem_limit_bytes=56 * 2**20
        ),
    )(lengths, queries, key_vectors, value_vectors, out_grad)


def solution(mesh):
    block = P("dp", "ctx", None)
    in_specs = (block, block, block, block, P("dp", None))
    out_specs = (block, P("dp", None, "ctx"), block, block, block)
    return jax.shard_map(attend, mesh=mesh, in_specs=in_specs, out_specs=out_specs, check_vma=False)
```

```python
import functools

import jax
import jax.numpy as jnp
from jax import lax
from jax.experimental import pallas as pl
from jax.experimental.pallas import tpu as pltpu
from jax.sharding import PartitionSpec as P

DH = 128
SPAN = 3
ROWS = 128
RING = 4
WINDOW = (SPAN + 1) * ROWS
CHUNKS = 4
AHEAD = 2
LOG2E = 1.4426950408889634
LN2 = 0.6931471805599453
MASKED = -1e30
MESH = pl.DeviceIdType.MESH

NT = (((1,), (1,)), ((), ()))
NN = (((1,), (0,)), ((), ()))
TN = (((0,), (0,)), ((), ()))


def dot(a, b, dims):
    return lax.dot_general(a, b, dims, preferred_element_type=jnp.float32)


def kernel(
    group,
    lengths,
    q_in,
    k_in,
    v_in,
    g_in,
    o_out,
    lse_out,
    dq_out,
    dk_out,
    dv_out,
    qb,
    kb,
    vb,
    gb,
    ob,
    dqb,
    lseb,
    own_k,
    own_v,
    far_k,
    far_v,
    near_k,
    near_v,
    fin_k,
    fin_v,
    bias,
    in_send,
    in_recv,
    halo_send,
    halo_recv,
    back_send,
    back_recv,
    out_send,
    out_recv,
    lse_send,
    lse_recv,
    in_local,
    out_local,
    lse_local,
):
    heads = group // DH
    width = group // CHUNKS
    per_chunk = width // DH
    dp = lax.axis_index("dp")
    ctx = lax.axis_index("ctx")
    z, x = ctx // RING, ctx % RING
    rings = lax.axis_size("ctx") // RING
    ahead = (dp, ((z + 1) % rings) * RING + x)
    behind = (dp, ((z + rings - 1) % rings) * RING + x)

    def at(step):
        return (x + step) % RING

    def peer(step):
        return (dp, z * RING + at(step))

    def span(start, size):
        return pl.ds(pl.multiple_of(start, DH), size)

    steps = (2, 1, 3)
    inputs = ((k_in, kb, SPAN), (v_in, vb, SPAN), (q_in, qb, 0), (g_in, gb, 0))

    barrier = pltpu.get_barrier_semaphore()
    for device in (peer(1), peer(2), peer(3), ahead, behind):
        pl.semaphore_signal(barrier, inc=1, device_id=device, device_id_type=MESH)
    pl.semaphore_wait(barrier, 5)

    def input_copy(c, a, step, sender):
        source, buffer, first = inputs[a]
        return pltpu.make_async_remote_copy(
            source.at[0, :, span(at(step) * group + c * width, width)],
            buffer.at[first + sender, :, span(c * width, width)],
            in_send.at[c, a, step - 1],
            in_recv.at[c, a, step - 1],
            device_id=peer(step),
            device_id_type=MESH,
        )

    def send_inputs(c):
        for a in range(4):
            for step in steps:
                input_copy(c, a, step, x).start()

    def wait_inputs(c, arrays):
        for a in arrays:
            for step in steps:
                input_copy(c, a, step, at(RING - step)).wait_recv()

    def local_input(a):
        source, buffer, first = inputs[a]
        return pltpu.make_async_copy(
            source.at[0, :, span(x * group, group)], buffer.at[first + x], in_local.at[a]
        )

    def halo_copy(c, a):
        buffer = (kb, vb)[a]
        columns = span(c * width, width)
        return pltpu.make_async_remote_copy(
            buffer.at[pl.ds(RING, SPAN), :, columns],
            buffer.at[pl.ds(0, SPAN), :, columns],
            halo_send.at[c, a],
            halo_recv.at[c, a],
            device_id=ahead,
            device_id_type=MESH,
        )

    def back_copy(c, a):
        columns = span(c * width, width)
        return pltpu.make_async_remote_copy(
            (far_k, far_v)[a].at[:, :, columns],
            (near_k, near_v)[a].at[:, :, columns],
            back_send.at[c, a],
            back_recv.at[c, a],
            device_id=behind,
            device_id_type=MESH,
        )

    outputs = ((ob, o_out), (dqb, dq_out), (fin_k, dk_out), (fin_v, dv_out))

    def output_copy(c, a, step):
        staged, out = outputs[a]
        return pltpu.make_async_remote_copy(
            staged.at[at(step), :, span(c * width, width)],
            out.at[0, :, span(x * group + c * width, width)],
            out_send.at[c, a, step - 1],
            out_recv.at[c, a, step - 1],
            device_id=peer(step),
            device_id_type=MESH,
        )

    def arrived_output(c, a, step):
        staged, out = outputs[a]
        return pltpu.make_async_remote_copy(
            staged.at[at(step), :, span(c * width, width)],
            out.at[0, :, span(at(RING - step) * group + c * width, width)],
            out_send.at[c, a, step - 1],
            out_recv.at[c, a, step - 1],
            device_id=peer(step),
            device_id_type=MESH,
        )

    def local_output(c, a):
        staged, out = outputs[a]
        return pltpu.make_async_copy(
            staged.at[x, :, span(c * width, width)],
            out.at[0, :, span(x * group + c * width, width)],
            out_local.at[c, a],
        )

    def send_outputs(c, arrays):
        for a in arrays:
            for step in steps:
                output_copy(c, a, step).start()
            local_output(c, a).start()

    def lse_copy(step, sender):
        return pltpu.make_async_remote_copy(
            lseb.at[at(step)],
            lse_out.at[0, pl.ds(pl.multiple_of(sender * heads, 8), heads), :],
            lse_send.at[step - 1],
            lse_recv.at[step - 1],
            device_id=peer(step),
            device_id_type=MESH,
        )

    for c in range(AHEAD):
        send_inputs(c)
    for a in range(4):
        local_input(a).start()

    for i in range(RING):
        base = (z * RING + i) * ROWS
        query_pos = base + lax.broadcasted_iota(jnp.int32, (1, ROWS), 1)
        first = jnp.zeros((1, ROWS), jnp.int32)
        start = jnp.int32(0)
        for d in range(lengths.shape[1]):
            first = jnp.where(start <= query_pos, start, first)
            start = start + lengths[0, d]
        key_pos = base - SPAN * ROWS + lax.broadcasted_iota(jnp.int32, (WINDOW, ROWS), 0)
        bias[i] = jnp.where((key_pos >= first) & (key_pos <= query_pos), 0.0, MASKED)

    for a in range(4):
        local_input(a).wait()

    scale = DH ** (-0.5)

    def one_head(h):
        columns = span(h * DH, DH)
        weights, slopes, query_blocks, grad_blocks = [], [], [], []
        for i in range(RING):
            keys = kb[i : i + SPAN + 1, :, columns].reshape(WINDOW, DH)
            values = vb[i : i + SPAN + 1, :, columns].reshape(WINDOW, DH)
            queries = qb[i, :, columns]
            grads = gb[i, :, columns]
            scores = dot(keys, queries, NT) * (scale * LOG2E) + bias[i]
            peak = jnp.max(scores, axis=0, keepdims=True)
            powers = jnp.exp2(scores - peak)
            totals = jnp.sum(powers, axis=0, keepdims=True)
            lseb[i, pl.ds(h, 1), :] = (peak + jnp.log2(totals)) * LN2
            weight = powers * (1.0 / totals)
            weight_low = weight.astype(jnp.bfloat16)
            pulls = dot(values, grads, NT)
            weighted = weight * pulls
            along = jnp.sum(weighted, axis=0, keepdims=True)
            slope = (weighted - weight * along).astype(jnp.bfloat16)
            ob[i, :, columns] = dot(weight_low, values, TN).astype(jnp.bfloat16)
            dqb[i, :, columns] = (dot(slope, keys, TN) * scale).astype(jnp.bfloat16)
            weights.append(weight_low)
            slopes.append(slope)
            query_blocks.append(queries)
            grad_blocks.append(grads)
        for j in range(SPAN + RING):
            seen = range(max(0, j - SPAN), min(RING - 1, j) + 1)

            def gather(parts):
                return jnp.concatenate(
                    [parts[i][(j - i) * ROWS : (j - i + 1) * ROWS] for i in seen], axis=1
                )

            def stack(blocks):
                return jnp.concatenate([blocks[i] for i in seen], axis=0)

            key_part = dot(gather(slopes), stack(query_blocks), NN) * scale
            value_part = dot(gather(weights), stack(grad_blocks), NN)
            if j < SPAN:
                far_k[j, :, columns] = key_part.astype(jnp.bfloat16)
                far_v[j, :, columns] = value_part.astype(jnp.bfloat16)
            else:
                own_k[j - SPAN, :, columns] = key_part
                own_v[j - SPAN, :, columns] = value_part

    def finish(c):
        columns = span(c * width, width)
        for a, (own, near, fin) in enumerate(
            ((own_k, near_k, fin_k), (own_v, near_v, fin_v))
        ):
            back_copy(c, a).wait_recv()
            fin[0, :, columns] = own[0, :, columns].astype(jnp.bfloat16)
            for s in range(1, RING):
                total = own[s, :, columns] + near[s - 1, :, columns].astype(jnp.float32)
                fin[s, :, columns] = total.astype(jnp.bfloat16)
        send_outputs(c, (2, 3))

    def one_chunk(c, carry):
        wait_inputs(c, (0, 1))
        for a in range(2):
            halo_copy(c, a).start()

        @pl.when(c + AHEAD < CHUNKS)
        def _():
            send_inputs(c + AHEAD)

        wait_inputs(c, (2, 3))
        for a in range(2):
            halo_copy(c, a).wait_recv()

        def head_step(h, inner):
            one_head(c * per_chunk + h)
            return inner

        lax.fori_loop(0, per_chunk, head_step, 0)
        for a in range(2):
            back_copy(c, a).start()
        send_outputs(c, (0, 1))

        @pl.when(c >= 1)
        def _():
            finish(c - 1)

        return carry

    lax.fori_loop(0, CHUNKS, one_chunk, 0)
    for step in steps:
        lse_copy(step, x).start()
    own_lse = pltpu.make_async_copy(
        lseb.at[x], lse_out.at[0, pl.ds(pl.multiple_of(x * heads, 8), heads), :], lse_local.at[0]
    )
    own_lse.start()
    finish(CHUNKS - 1)

    def drain(c, carry):
        for a in range(2):
            halo_copy(c, a).wait_send()
            back_copy(c, a).wait_send()
        for a in range(4):
            local_output(c, a).wait()
            for step in steps:
                input_copy(c, a, step, x).wait_send()
                output_copy(c, a, step).wait_send()
                arrived_output(c, a, step).wait_recv()
        return carry

    lax.fori_loop(0, CHUNKS, drain, 0)
    own_lse.wait()
    for step in steps:
        lse_copy(step, x).wait_send()
        lse_copy(step, at(RING - step)).wait_recv()


def write_out(*refs):
    sems = refs[10]
    moves = [pltpu.make_async_copy(refs[i], refs[5 + i], sems.at[i]) for i in range(5)]
    for move in moves:
        move.start()
    for move in moves:
        move.wait()


def attend(queries, key_vectors, value_vectors, out_grad, lengths):
    _, rows, all_width = queries.shape
    group = all_width // RING
    heads = group // DH
    block = pltpu.VMEM(queries.shape, jnp.bfloat16)
    totals = pltpu.VMEM((1, all_width // DH, rows), jnp.float32)
    anywhere = pl.BlockSpec(memory_space=pl.ANY)
    low = functools.partial(pltpu.VMEM, dtype=jnp.bfloat16)
    wide = functools.partial(pltpu.VMEM, dtype=jnp.float32)
    copies = pltpu.SemaphoreType.DMA
    results = pl.pallas_call(
        functools.partial(kernel, group),
        name="spread_heads_attention",
        out_shape=(block, totals, block, block, block),
        in_specs=[pl.BlockSpec(memory_space=pltpu.SMEM)] + [anywhere] * 4,
        out_specs=(pl.BlockSpec(memory_space=pltpu.VMEM),) * 5,
        scratch_shapes=[
            low((RING, rows, group)),
            low((SPAN + RING, rows, group)),
            low((SPAN + RING, rows, group)),
            low((RING, rows, group)),
            low((RING, rows, group)),
            low((RING, rows, group)),
            wide((RING, heads, rows)),
            wide((RING, rows, group)),
            wide((RING, rows, group)),
            low((SPAN, rows, group)),
            low((SPAN, rows, group)),
            low((SPAN, rows, group)),
            low((SPAN, rows, group)),
            low((RING, rows, group)),
            low((RING, rows, group)),
            wide((RING, WINDOW, ROWS)),
            copies((CHUNKS, 4, 3)),
            copies((CHUNKS, 4, 3)),
            copies((CHUNKS, 2)),
            copies((CHUNKS, 2)),
            copies((CHUNKS, 2)),
            copies((CHUNKS, 2)),
            copies((CHUNKS, 4, 3)),
            copies((CHUNKS, 4, 3)),
            copies((3,)),
            copies((3,)),
            copies((4,)),
            copies((CHUNKS, 4)),
            copies((1,)),
        ],
        compiler_params=pltpu.CompilerParams(
            collective_id=0, has_side_effects=True, vmem_limit_bytes=48 * 2**20
        ),
    )(lengths, queries, key_vectors, value_vectors, out_grad)
    return pl.pallas_call(
        write_out,
        name="write_out",
        out_shape=tuple(jax.ShapeDtypeStruct(r.shape, r.dtype) for r in results),
        in_specs=[pl.BlockSpec(memory_space=pltpu.VMEM)] * 5,
        out_specs=(anywhere,) * 5,
        scratch_shapes=[copies((5,))],
    )(*results)


def solution(mesh):
    block = P("dp", "ctx", None)
    in_specs = (block, block, block, block, P("dp", None))
    out_specs = (block, P("dp", None, "ctx"), block, block, block)
    return jax.shard_map(attend, mesh=mesh, in_specs=in_specs, out_specs=out_specs, check_vma=False)
```

```python
import functools

import jax
import jax.numpy as jnp
from jax import lax
from jax.experimental import pallas as pl
from jax.experimental.pallas import tpu as pltpu
from jax.sharding import PartitionSpec as P

DH = 128
SPAN = 3
ROWS = 128
RING = 4
WINDOW = (SPAN + 1) * ROWS
CHUNKS = 4
AHEAD = 2
LOG2E = 1.4426950408889634
LN2 = 0.6931471805599453
MASKED = -1e30
MESH = pl.DeviceIdType.MESH

NT = (((1,), (1,)), ((), ()))
NN = (((1,), (0,)), ((), ()))
TN = (((0,), (0,)), ((), ()))


def dot(a, b, dims):
    return lax.dot_general(a, b, dims, preferred_element_type=jnp.float32)


def kernel(
    group,
    lengths,
    q_in,
    k_in,
    v_in,
    g_in,
    o_out,
    lse_out,
    dq_out,
    dk_out,
    dv_out,
    qb,
    kb,
    vb,
    gb,
    ob,
    dqb,
    lseb,
    own_k,
    own_v,
    far_k,
    far_v,
    near_k,
    near_v,
    fin_k,
    fin_v,
    bias,
    in_send,
    in_recv,
    halo_send,
    halo_recv,
    back_send,
    back_recv,
    out_send,
    out_recv,
    lse_send,
    lse_recv,
    in_local,
    out_local,
    lse_local,
):
    heads = group // DH
    width = group // CHUNKS
    per_chunk = width // DH
    dp = lax.axis_index("dp")
    ctx = lax.axis_index("ctx")
    z, x = ctx // RING, ctx % RING
    rings = lax.axis_size("ctx") // RING
    ahead = (dp, ((z + 1) % rings) * RING + x)
    behind = (dp, ((z + rings - 1) % rings) * RING + x)

    def at(step):
        return (x + step) % RING

    def peer(step):
        return (dp, z * RING + at(step))

    def span(start, size):
        return pl.ds(pl.multiple_of(start, DH), size)

    steps = (2, 1, 3)
    inputs = ((k_in, kb, SPAN), (v_in, vb, SPAN), (q_in, qb, 0), (g_in, gb, 0))

    barrier = pltpu.get_barrier_semaphore()
    for device in (peer(1), peer(2), peer(3), ahead, behind):
        pl.semaphore_signal(barrier, inc=1, device_id=device, device_id_type=MESH)
    pl.semaphore_wait(barrier, 5)

    def input_copy(c, a, step, sender):
        source, buffer, first = inputs[a]
        return pltpu.make_async_remote_copy(
            source.at[0, :, span(at(step) * group + c * width, width)],
            buffer.at[first + sender, :, span(c * width, width)],
            in_send.at[c, a, step - 1],
            in_recv.at[c, a, step - 1],
            device_id=peer(step),
            device_id_type=MESH,
        )

    def send_inputs(c):
        for a in range(4):
            for step in steps:
                input_copy(c, a, step, x).start()

    def wait_inputs(c, arrays):
        for a in arrays:
            for step in steps:
                input_copy(c, a, step, at(RING - step)).wait_recv()

    def local_input(a):
        source, buffer, first = inputs[a]
        return pltpu.make_async_copy(
            source.at[0, :, span(x * group, group)], buffer.at[first + x], in_local.at[a]
        )

    def halo_copy(c, a):
        buffer = (kb, vb)[a]
        columns = span(c * width, width)
        return pltpu.make_async_remote_copy(
            buffer.at[pl.ds(RING, SPAN), :, columns],
            buffer.at[pl.ds(0, SPAN), :, columns],
            halo_send.at[c, a],
            halo_recv.at[c, a],
            device_id=ahead,
            device_id_type=MESH,
        )

    def back_copy(c, a):
        columns = span(c * width, width)
        return pltpu.make_async_remote_copy(
            (far_k, far_v)[a].at[:, :, columns],
            (near_k, near_v)[a].at[:, :, columns],
            back_send.at[c, a],
            back_recv.at[c, a],
            device_id=behind,
            device_id_type=MESH,
        )

    outputs = ((ob, o_out), (dqb, dq_out), (fin_k, dk_out), (fin_v, dv_out))

    def output_copy(c, a, step):
        staged, out = outputs[a]
        return pltpu.make_async_remote_copy(
            staged.at[at(step), :, span(c * width, width)],
            out.at[0, :, span(x * group + c * width, width)],
            out_send.at[c, a, step - 1],
            out_recv.at[c, a, step - 1],
            device_id=peer(step),
            device_id_type=MESH,
        )

    def arrived_output(c, a, step):
        staged, out = outputs[a]
        return pltpu.make_async_remote_copy(
            staged.at[at(step), :, span(c * width, width)],
            out.at[0, :, span(at(RING - step) * group + c * width, width)],
            out_send.at[c, a, step - 1],
            out_recv.at[c, a, step - 1],
            device_id=peer(step),
            device_id_type=MESH,
        )

    def local_output(c, a):
        staged, out = outputs[a]
        return pltpu.make_async_copy(
            staged.at[x, :, span(c * width, width)],
            out.at[0, :, span(x * group + c * width, width)],
            out_local.at[c, a],
        )

    def send_outputs(c, arrays):
        for a in arrays:
            for step in steps:
                output_copy(c, a, step).start()
            local_output(c, a).start()

    def lse_copy(step, sender):
        return pltpu.make_async_remote_copy(
            lseb.at[at(step)],
            lse_out.at[0, pl.ds(pl.multiple_of(sender * heads, 8), heads), :],
            lse_send.at[step - 1],
            lse_recv.at[step - 1],
            device_id=peer(step),
            device_id_type=MESH,
        )

    for c in range(AHEAD):
        send_inputs(c)
    for a in range(4):
        local_input(a).start()

    for i in range(RING):
        base = (z * RING + i) * ROWS
        query_pos = base + lax.broadcasted_iota(jnp.int32, (1, ROWS), 1)
        first = jnp.zeros((1, ROWS), jnp.int32)
        start = jnp.int32(0)
        for d in range(lengths.shape[1]):
            first = jnp.where(start <= query_pos, start, first)
            start = start + lengths[0, d]
        key_pos = base - SPAN * ROWS + lax.broadcasted_iota(jnp.int32, (WINDOW, ROWS), 0)
        bias[i] = jnp.where((key_pos >= first) & (key_pos <= query_pos), 0.0, MASKED)

    for a in range(4):
        local_input(a).wait()

    scale = DH ** (-0.5)

    def one_head(h):
        columns = span(h * DH, DH)
        weights, slopes, query_blocks, grad_blocks = [], [], [], []
        for i in range(RING):
            keys = kb[i : i + SPAN + 1, :, columns].reshape(WINDOW, DH)
            values = vb[i : i + SPAN + 1, :, columns].reshape(WINDOW, DH)
            queries = qb[i, :, columns]
            grads = gb[i, :, columns]
            scores = dot(keys, queries, NT) * (scale * LOG2E) + bias[i]
            peak = jnp.max(scores, axis=0, keepdims=True)
            powers = jnp.exp2(scores - peak)
            totals = jnp.sum(powers, axis=0, keepdims=True)
            lseb[i, pl.ds(h, 1), :] = (peak + jnp.log2(totals)) * LN2
            weight = powers * (1.0 / totals)
            weight_low = weight.astype(jnp.bfloat16)
            pulls = dot(values, grads, NT)
            weighted = weight * pulls
            along = jnp.sum(weighted, axis=0, keepdims=True)
            slope = (weighted - weight * along).astype(jnp.bfloat16)
            ob[i, :, columns] = dot(weight_low, values, TN).astype(jnp.bfloat16)
            dqb[i, :, columns] = (dot(slope, keys, TN) * scale).astype(jnp.bfloat16)
            weights.append(weight_low)
            slopes.append(slope)
            query_blocks.append(queries)
            grad_blocks.append(grads)
        for j in range(SPAN + RING):
            seen = range(max(0, j - SPAN), min(RING - 1, j) + 1)

            def gather(parts):
                return jnp.concatenate(
                    [parts[i][(j - i) * ROWS : (j - i + 1) * ROWS] for i in seen], axis=1
                )

            def stack(blocks):
                return jnp.concatenate([blocks[i] for i in seen], axis=0)

            key_part = dot(gather(slopes), stack(query_blocks), NN) * scale
            value_part = dot(gather(weights), stack(grad_blocks), NN)
            if j < SPAN:
                far_k[j, :, columns] = key_part.astype(jnp.bfloat16)
                far_v[j, :, columns] = value_part.astype(jnp.bfloat16)
            else:
                own_k[j - SPAN, :, columns] = key_part
                own_v[j - SPAN, :, columns] = value_part

    def finish(c):
        columns = span(c * width, width)
        for a, (own, near, fin) in enumerate(
            ((own_k, near_k, fin_k), (own_v, near_v, fin_v))
        ):
            back_copy(c, a).wait_recv()
            fin[0, :, columns] = own[0, :, columns].astype(jnp.bfloat16)
            for s in range(1, RING):
                total = own[s, :, columns] + near[s - 1, :, columns].astype(jnp.float32)
                fin[s, :, columns] = total.astype(jnp.bfloat16)
        send_outputs(c, (2, 3))

    def one_chunk(c, carry):
        wait_inputs(c, (0, 1))
        for a in range(2):
            halo_copy(c, a).start()

        @pl.when(c + AHEAD < CHUNKS)
        def _():
            send_inputs(c + AHEAD)

        wait_inputs(c, (2, 3))
        for a in range(2):
            halo_copy(c, a).wait_recv()

        def head_step(h, inner):
            one_head(c * per_chunk + h)
            return inner

        lax.fori_loop(0, per_chunk, head_step, 0)
        for a in range(2):
            back_copy(c, a).start()
        send_outputs(c, (0, 1))

        @pl.when(c >= 1)
        def _():
            finish(c - 1)

        return carry

    lax.fori_loop(0, CHUNKS, one_chunk, 0)
    for step in steps:
        lse_copy(step, x).start()
    own_lse = pltpu.make_async_copy(
        lseb.at[x], lse_out.at[0, pl.ds(pl.multiple_of(x * heads, 8), heads), :], lse_local.at[0]
    )
    own_lse.start()
    finish(CHUNKS - 1)

    def drain(c, carry):
        for a in range(2):
            halo_copy(c, a).wait_send()
            back_copy(c, a).wait_send()
        for a in range(4):
            local_output(c, a).wait()
            for step in steps:
                input_copy(c, a, step, x).wait_send()
                output_copy(c, a, step).wait_send()
                arrived_output(c, a, step).wait_recv()
        return carry

    lax.fori_loop(0, CHUNKS, drain, 0)
    own_lse.wait()
    for step in steps:
        lse_copy(step, x).wait_send()
        lse_copy(step, at(RING - step)).wait_recv()


def write_out(*refs):
    sems = refs[10]
    moves = [pltpu.make_async_copy(refs[i], refs[5 + i], sems.at[i]) for i in range(5)]
    for move in moves:
        move.start()
    for move in moves:
        move.wait()


def write_results(*results):
    return pl.pallas_call(
        write_out,
        name="write_out",
        out_shape=tuple(jax.ShapeDtypeStruct(r.shape, r.dtype) for r in results),
        in_specs=[pl.BlockSpec(memory_space=pltpu.VMEM)] * 5,
        out_specs=(pl.BlockSpec(memory_space=pl.ANY),) * 5,
        scratch_shapes=[pltpu.SemaphoreType.DMA((5,))],
        compiler_params=pltpu.CompilerParams(vmem_limit_bytes=2**20),
    )(*(pltpu.with_memory_space_constraint(r, pltpu.VMEM) for r in results))


def attend(queries, key_vectors, value_vectors, out_grad, lengths):
    _, rows, all_width = queries.shape
    group = all_width // RING
    heads = group // DH
    block = pltpu.VMEM(queries.shape, jnp.bfloat16)
    totals = pltpu.VMEM((1, all_width // DH, rows), jnp.float32)
    anywhere = pl.BlockSpec(memory_space=pl.ANY)
    low = functools.partial(pltpu.VMEM, dtype=jnp.bfloat16)
    wide = functools.partial(pltpu.VMEM, dtype=jnp.float32)
    copies = pltpu.SemaphoreType.DMA
    results = pl.pallas_call(
        functools.partial(kernel, group),
        name="spread_heads_attention",
        out_shape=(block, totals, block, block, block),
        in_specs=[pl.BlockSpec(memory_space=pltpu.SMEM)] + [anywhere] * 4,
        out_specs=(pl.BlockSpec(memory_space=pltpu.VMEM),) * 5,
        scratch_shapes=[
            low((RING, rows, group)),
            low((SPAN + RING, rows, group)),
            low((SPAN + RING, rows, group)),
            low((RING, rows, group)),
            low((RING, rows, group)),
            low((RING, rows, group)),
            wide((RING, heads, rows)),
            wide((RING, rows, group)),
            wide((RING, rows, group)),
            low((SPAN, rows, group)),
            low((SPAN, rows, group)),
            low((SPAN, rows, group)),
            low((SPAN, rows, group)),
            low((RING, rows, group)),
            low((RING, rows, group)),
            wide((RING, WINDOW, ROWS)),
            copies((CHUNKS, 4, 3)),
            copies((CHUNKS, 4, 3)),
            copies((CHUNKS, 2)),
            copies((CHUNKS, 2)),
            copies((CHUNKS, 2)),
            copies((CHUNKS, 2)),
            copies((CHUNKS, 4, 3)),
            copies((CHUNKS, 4, 3)),
            copies((3,)),
            copies((3,)),
            copies((4,)),
            copies((CHUNKS, 4)),
            copies((1,)),
        ],
        compiler_params=pltpu.CompilerParams(
            collective_id=0, has_side_effects=True, vmem_limit_bytes=48 * 2**20
        ),
    )(lengths, queries, key_vectors, value_vectors, out_grad)
    return write_results(*results)


def solution(mesh):
    block = P("dp", "ctx", None)
    in_specs = (block, block, block, block, P("dp", None))
    out_specs = (block, P("dp", None, "ctx"), block, block, block)
    return jax.shard_map(attend, mesh=mesh, in_specs=in_specs, out_specs=out_specs, check_vma=False)
```

```python
import functools

import jax
import jax.numpy as jnp
from jax import lax
from jax.experimental import pallas as pl
from jax.experimental.pallas import tpu as pltpu
from jax.sharding import PartitionSpec as P

DH = 128
ROWS = 128
HALF = 64
LONGEST = 384
COVER = LONGEST // 2
KEYS = COVER + ROWS
QUERIES = 3 * ROWS
HEADS = 2
AHEAD = 3
DEPTH = 1
PATIENCE = 1
TURN = DEPTH + PATIENCE + 1
LAG = TURN + DEPTH + AHEAD
SLOTS = AHEAD + 1
LOG2E = 1.4426950408889634
LN2 = 0.6931471805599453
MASKED = -1e30
NEVER = 1 << 30
MESH = pl.DeviceIdType.MESH

NT = (((1,), (1,)), ((), ()))
NN = (((1,), (0,)), ((), ()))
TN = (((0,), (0,)), ((), ()))


def dot(a, b, dims):
    return lax.dot_general(a, b, dims, preferred_element_type=jnp.float32)


def kernel(
    lengths,
    q_in,
    k_in,
    v_in,
    g_in,
    o_out,
    lse_out,
    dq_out,
    dk_out,
    dv_out,
    q_all,
    k_all,
    v_all,
    g_all,
    right1,
    right2,
    left1,
    left2,
    from_left1,
    from_left2,
    from_right1,
    from_right2,
    far_q1,
    far_q2,
    far_k1,
    far_k2,
    own_q,
    own_k,
    powers,
    pulls,
    peaks,
    stats,
    stats_left1,
    stats_left2,
    stats_right1,
    stats_right2,
    bias,
    in_local,
    msg_send,
    msg_recv,
    stat_send,
    stat_recv,
):
    width = HEADS * DH
    chunks = q_all.shape[1] // width
    steps = chunks + LAG
    spare = chunks + TURN
    blocks = lax.axis_size("ctx")
    dp = lax.axis_index("dp")
    me = lax.axis_index("ctx")

    def device(step):
        return (dp, (me + step + blocks) % blocks)

    def span(c):
        return pl.ds(pl.multiple_of(c * width, width), width)

    early = 8 * DH
    loads = [
        [
            pltpu.make_async_copy(source.at[0, :, part], kept.at[:, part], in_local.at[p, i])
            for i, (source, kept) in enumerate(
                ((k_in, k_all), (v_in, v_all), (q_in, q_all), (g_in, g_all))
            )
        ]
        for p, part in enumerate((slice(0, early), slice(early, q_all.shape[1])))
    ]
    for load in loads[0] + loads[1]:
        load.start()
    barrier = pltpu.get_barrier_semaphore()
    for step in (1, 2, -1, -2):
        pl.semaphore_signal(barrier, inc=1, device_id=device(step), device_id_type=MESH)

    last = blocks * ROWS

    def document_start(position):
        first = position * 0
        start = jnp.int32(0)
        for d in range(lengths.shape[1]):
            first = jnp.where(start <= position, start, first)
            start = start + lengths[0, d]
        return first

    def keys_cross(block):
        edge = block * ROWS
        return (edge - document_start(edge) <= COVER) | (edge >= last)

    keys0, keys1 = keys_cross(me), keys_cross(me + 1)

    for load in loads[0]:
        load.wait()
    pl.semaphore_wait(barrier, 4)

    routes = (
        (right1, from_left1, 1),
        (left1, from_right1, -1),
        (right2, from_left2, 1),
        (left2, from_right2, -1),
    )

    def message(s, i):
        staged, landed, step = routes[i]
        slot = s % SLOTS
        return pltpu.make_async_remote_copy(
            staged.at[slot],
            landed.at[s],
            msg_send.at[slot, i],
            msg_recv.at[s, i],
            device_id=device(step),
            device_id_type=MESH,
        )

    def start(s, which):
        for i in which:
            message(s, i).start()

    def reuse(s, which):
        @pl.when(s >= SLOTS)
        def _():
            for i in which:
                message(s - SLOTS, i).wait_send()

    def send_blocks(s):
        slot = s % SLOTS
        columns = span(jnp.minimum(s, chunks - 1))
        keep = (s + 3 * LAG) % 4
        back = jnp.where(s >= LAG, s - LAG + TURN, spare)
        reuse(s, (0, 1))
        for a, (own_key, own_query) in enumerate(((k_all, q_all), (v_all, g_all))):
            more = from_left2[back, a].astype(jnp.float32)
            more = jnp.where(keys0, 0.0, more)
            head = (far_q1[keep, a, :HALF] + more).astype(jnp.bfloat16)
            tail = far_q1[keep, a, HALF:].astype(jnp.bfloat16)
            right1[slot, a, :HALF] = jnp.where(keys1, own_key[:HALF, columns], head)
            right1[slot, a, HALF:] = jnp.where(keys1, own_key[HALF:, columns], tail)
            more = from_right2[back, a].astype(jnp.float32)
            more = jnp.where(keys1, more, 0.0)
            head = far_k1[keep, a, :HALF].astype(jnp.bfloat16)
            tail = (far_k1[keep, a, HALF:] + more).astype(jnp.bfloat16)
            left1[slot, a, :HALF] = jnp.where(keys0, head, own_query[:HALF, columns])
            left1[slot, a, HALF:] = jnp.where(keys0, tail, own_query[HALF:, columns])
        start(s, (0, 1))

    def send_halves(s):
        slot = s % SLOTS
        done = (s + TURN) % 2
        reuse(s, (2, 3))
        for a in range(2):
            right2[slot, a] = jnp.where(keys1, from_left1[s, a, ROWS - HALF :], far_q2[done, a])
            left2[slot, a] = jnp.where(keys0, far_k2[done, a], from_right1[s, a, :HALF])
        start(s, (2, 3))

    stat_routes = (
        (slice(ROWS, 3 * ROWS), stats_left1, 1),
        (slice(0, 2 * ROWS), stats_right1, -1),
        (slice(2 * ROWS, 3 * ROWS), stats_left2, 2),
        (slice(0, ROWS), stats_right2, -2),
    )

    def stat_message(c, i):
        lanes, landed, step = stat_routes[i]
        return pltpu.make_async_remote_copy(
            stats.at[c, :, lanes],
            landed.at[c],
            stat_send.at[c, i],
            stat_recv.at[c, i],
            device_id=device(step),
            device_id_type=MESH,
        )

    scale = DH ** (-0.5)
    pad = jnp.zeros((ROWS - HALF, DH), jnp.bfloat16)

    def met_keys(c, a, h):
        inner = slice(h * DH, (h + 1) * DH)
        own = (k_all, v_all)[a][:, pl.ds(pl.multiple_of(c * width + h * DH, DH), DH)]
        return jnp.concatenate(
            [from_left2[c, a, :, inner], from_left1[c, a, :, inner], own], axis=0
        )

    def met_queries(c, a, h):
        inner = slice(h * DH, (h + 1) * DH)
        own = (q_all, g_all)[a][:, pl.ds(pl.multiple_of(c * width + h * DH, DH), DH)]
        return jnp.concatenate(
            [own, from_right1[c, a, :, inner], from_right2[c, a, :, inner], pad], axis=0
        )

    def partial_totals(c):
        slot = c % (PATIENCE + 1)
        for h in range(HEADS):
            score = dot(met_keys(c, 0, h), met_queries(c, 0, h), NT) * (scale * LOG2E) + bias[...]
            pull = dot(met_keys(c, 1, h), met_queries(c, 1, h), NT)
            pulls[slot, h] = pull
            peak = jnp.max(score, axis=0, keepdims=True)
            power = jnp.exp2(score - peak)
            powers[slot, h] = power
            peaks[slot, pl.ds(h, 1), :] = peak
            total = jnp.sum(power, axis=0, keepdims=True)
            along = jnp.sum(power * pull, axis=0, keepdims=True) / total
            stats[c, pl.ds(2 * h, 1), :] = peak + jnp.log2(total)
            stats[c, pl.ds(2 * h + 1, 1), :] = along
        for i in range(4):
            stat_message(c, i).start()

    def gradients(c):
        slot, done = c % (PATIENCE + 1), c % 2
        keep, turn = c % 8, c % 4
        for i in range(4):
            stat_message(c, i).wait_recv()
        mine = stats[c]
        left, right = stats_left1[c], stats_right1[c]
        second = jnp.concatenate([left, right[:, ROWS:]], axis=1)
        third = jnp.concatenate([stats_left2[c], right[:, :ROWS], stats_right2[c]], axis=1)
        for h in range(HEADS):
            inner = slice(h * DH, (h + 1) * DH)
            logs = [part[2 * h : 2 * h + 1] for part in (mine, second, third)]
            peak = jnp.maximum(jnp.maximum(logs[0], logs[1]), logs[2])
            shares = [jnp.exp2(log - peak) for log in logs]
            total = shares[0] + shares[1] + shares[2]
            log_total = peak + jnp.log2(total)
            along = sum(
                share * part[2 * h + 1 : 2 * h + 2]
                for share, part in zip(shares, (mine, second, third))
            ) / total
            lse_out[0, pl.ds(c * HEADS + h, 1), :] = log_total[:, :ROWS] * LN2
            weight = powers[slot, h] * jnp.exp2(peaks[slot, pl.ds(h, 1), :] - log_total)
            slope = (weight * (pulls[slot, h] - along)).astype(jnp.bfloat16)
            weight = weight.astype(jnp.bfloat16)
            keys, values = met_keys(c, 0, h), met_keys(c, 1, h)
            queries, grads = met_queries(c, 0, h), met_queries(c, 1, h)
            for a, (query_part, key_part) in enumerate(
                (
                    (dot(weight, values, TN), dot(slope, queries, NN) * scale),
                    (dot(slope, keys, TN) * scale, dot(weight, grads, NN)),
                )
            ):
                own_q[keep, a, :, inner] = query_part[:ROWS]
                far_q1[turn, a, :, inner] = query_part[ROWS : 2 * ROWS]
                far_q2[done, a, :, inner] = query_part[2 * ROWS : 2 * ROWS + HALF].astype(
                    jnp.bfloat16
                )
                own_k[keep, a, :, inner] = key_part[COVER:]
                far_k1[turn, a, :, inner] = key_part[HALF:COVER]
                far_k2[done, a, :, inner] = key_part[:HALF].astype(jnp.bfloat16)

    def finish(s):
        c = s - LAG
        keep = c % 8
        columns = span(c)
        for a, (query_out, key_out) in enumerate(((o_out, dk_out), (dq_out, dv_out))):
            query_part = jnp.where(keys0, 0.0, from_left1[s, a].astype(jnp.float32))
            query_out[0, :, columns] = (own_q[keep, a] + query_part).astype(jnp.bfloat16)
            key_part = jnp.where(keys1, from_right1[s, a].astype(jnp.float32), 0.0)
            key_out[0, :, columns] = (own_k[keep, a] + key_part).astype(jnp.bfloat16)

    for far in (far_q1, far_q2, far_k1, far_k2):
        far[...] = jnp.zeros(far.shape, far.dtype)
    for landed in (from_left2, from_right2):
        landed[spare] = jnp.zeros(landed.shape[1:], landed.dtype)
    for s in range(AHEAD):
        send_blocks(s)

    query_pos = me * ROWS + lax.broadcasted_iota(jnp.int32, (1, QUERIES), 1)
    first = document_start(query_pos)
    lane = lax.broadcasted_iota(jnp.int32, (1, QUERIES), 1)
    first = jnp.where((query_pos >= last) | (lane >= 2 * ROWS + HALF), NEVER, first)
    first = jnp.where((lane >= ROWS) & (lane * 0 + keys1.astype(jnp.int32) > 0), NEVER, first)
    key_pos = me * ROWS - COVER + lax.broadcasted_iota(jnp.int32, (KEYS, 1), 0)
    seen_pos = jnp.where(
        (key_pos < me * ROWS) & (key_pos * 0 + keys0.astype(jnp.int32) == 0), -1, key_pos
    )
    bias[...] = jnp.where((seen_pos >= first) & (key_pos <= query_pos), 0.0, MASKED)

    for load in loads[1]:
        load.wait()

    def one_step(s, carry):
        for i in (0, 1):
            message(s, i).wait_recv()

        @pl.when(s < chunks + TURN)
        def _():
            send_halves(s)

        @pl.when((s >= DEPTH) & (s < chunks + TURN + DEPTH))
        def _():
            for i in (2, 3):
                message(s - DEPTH, i).wait_recv()

        @pl.when((s >= DEPTH) & (s < chunks + DEPTH))
        def _():
            partial_totals(s - DEPTH)

        @pl.when(s + AHEAD < steps)
        def _():
            send_blocks(s + AHEAD)

        @pl.when((s >= DEPTH + PATIENCE) & (s < chunks + DEPTH + PATIENCE))
        def _():
            gradients(s - DEPTH - PATIENCE)

        @pl.when(s >= LAG)
        def _():
            finish(s)

        return carry

    lax.fori_loop(0, steps, one_step, 0)
    for which, count in (((0, 1), steps), ((2, 3), chunks + TURN)):
        for s in range(count - SLOTS, count):
            for i in which:
                message(s, i).wait_send()

    def drain(c, carry):
        for i in range(4):
            stat_message(c, i).wait_send()
        return carry

    lax.fori_loop(0, chunks, drain, 0)


def write_out(*refs):
    sems = refs[10]
    moves = [pltpu.make_async_copy(refs[i], refs[5 + i], sems.at[i]) for i in range(5)]
    for move in moves:
        move.start()
    for move in moves:
        move.wait()


def write_results(*results):
    return pl.pallas_call(
        write_out,
        name="write_out",
        out_shape=tuple(jax.ShapeDtypeStruct(r.shape, r.dtype) for r in results),
        in_specs=[pl.BlockSpec(memory_space=pltpu.VMEM)] * 5,
        out_specs=(pl.BlockSpec(memory_space=pl.ANY),) * 5,
        scratch_shapes=[pltpu.SemaphoreType.DMA((5,))],
        compiler_params=pltpu.CompilerParams(vmem_limit_bytes=2**20),
    )(*(pltpu.with_memory_space_constraint(r, pltpu.VMEM) for r in results))


def attend(queries, key_vectors, value_vectors, out_grad, lengths):
    _, rows, all_width = queries.shape
    heads = all_width // DH
    width = HEADS * DH
    chunks = heads // HEADS
    steps = chunks + LAG
    block = pltpu.VMEM(queries.shape, jnp.bfloat16)
    totals = pltpu.VMEM((1, heads, rows), jnp.float32)
    anywhere = pl.BlockSpec(memory_space=pl.ANY)
    low = functools.partial(pltpu.VMEM, dtype=jnp.bfloat16)
    wide = functools.partial(pltpu.VMEM, dtype=jnp.float32)
    copies = pltpu.SemaphoreType.DMA
    results = pl.pallas_call(
        kernel,
        name="chain_attention",
        out_shape=(block, totals, block, block, block),
        in_specs=[pl.BlockSpec(memory_space=pltpu.SMEM)] + [anywhere] * 4,
        out_specs=(pl.BlockSpec(memory_space=pltpu.VMEM),) * 5,
        scratch_shapes=[low((rows, all_width))] * 4
        + [low((SLOTS, 2, ROWS, width)), low((SLOTS, 2, HALF, width))] * 2
        + [low((steps, 2, ROWS, width)), low((chunks + TURN + 1, 2, HALF, width))] * 2
        + [wide((4, 2, ROWS, width)), low((2, 2, HALF, width))] * 2
        + [
            wide((8, 2, ROWS, width)),
            wide((8, 2, ROWS, width)),
            wide((PATIENCE + 1, HEADS, KEYS, QUERIES)),
            wide((PATIENCE + 1, HEADS, KEYS, QUERIES)),
            wide((PATIENCE + 1, HEADS, QUERIES)),
            wide((chunks, 2 * HEADS, QUERIES)),
            wide((chunks, 2 * HEADS, 2 * ROWS)),
            wide((chunks, 2 * HEADS, ROWS)),
            wide((chunks, 2 * HEADS, 2 * ROWS)),
            wide((chunks, 2 * HEADS, ROWS)),
            wide((KEYS, QUERIES)),
            copies((2, 4)),
            copies((SLOTS, 4)),
            copies((steps, 4)),
            copies((chunks, 4)),
            copies((chunks, 4)),
        ],
        compiler_params=pltpu.CompilerParams(
            collective_id=0, has_side_effects=True, vmem_limit_bytes=48 * 2**20
        ),
    )(lengths, queries, key_vectors, value_vectors, out_grad)
    return write_results(*results)


def solution(mesh):
    block = P("dp", "ctx", None)
    in_specs = (block, block, block, block, P("dp", None))
    out_specs = (block, P("dp", None, "ctx"), block, block, block)
    return jax.shard_map(attend, mesh=mesh, in_specs=in_specs, out_specs=out_specs, check_vma=False)
```

```python
import functools

import jax
import jax.numpy as jnp
from jax import lax
from jax.experimental import pallas as pl
from jax.experimental.pallas import tpu as pltpu
from jax.sharding import PartitionSpec as P

DH = 128
ROWS = 128
HALF = 64
LONGEST = 384
COVER = LONGEST // 2
KEYS = COVER + ROWS
QUERIES = 3 * ROWS
HEADS = 2
AHEAD = 3
DEPTH = 1
PATIENCE = 1
TURN = DEPTH + PATIENCE + 1
LAG = TURN + DEPTH + AHEAD
SLOTS = AHEAD + 1
LOG2E = 1.4426950408889634
LN2 = 0.6931471805599453
MASKED = -1e30
NEVER = 1 << 30
MESH = pl.DeviceIdType.MESH

NT = (((1,), (1,)), ((), ()))
NN = (((1,), (0,)), ((), ()))
TN = (((0,), (0,)), ((), ()))


def dot(a, b, dims):
    return lax.dot_general(a, b, dims, preferred_element_type=jnp.float32)


def kernel(
    lengths,
    q_in,
    k_in,
    v_in,
    g_in,
    o_out,
    lse_out,
    dq_out,
    dk_out,
    dv_out,
    q_all,
    k_all,
    v_all,
    g_all,
    right1,
    right2,
    left1,
    left2,
    from_left1,
    from_left2,
    from_right1,
    from_right2,
    far_q1,
    far_q2,
    far_k1,
    far_k2,
    own_q,
    own_k,
    powers,
    pulls,
    peaks,
    stats,
    to_left1,
    to_left2,
    to_right1,
    to_right2,
    stats_left1,
    stats_left2,
    stats_right1,
    stats_right2,
    bias,
    in_local,
    msg_send,
    msg_recv,
    stat_send,
    stat_recv,
):
    width = HEADS * DH
    chunks = q_all.shape[1] // width
    steps = chunks + LAG
    spare = chunks + TURN
    blocks = lax.axis_size("ctx")
    dp = lax.axis_index("dp")
    me = lax.axis_index("ctx")

    def device(step):
        return (dp, (me + step + blocks) % blocks)

    def span(c):
        return pl.ds(pl.multiple_of(c * width, width), width)

    early = 8 * DH
    loads = [
        [
            pltpu.make_async_copy(source.at[0, :, part], kept.at[:, part], in_local.at[p, i])
            for i, (source, kept) in enumerate(
                ((k_in, k_all), (v_in, v_all), (q_in, q_all), (g_in, g_all))
            )
        ]
        for p, part in enumerate((slice(0, early), slice(early, q_all.shape[1])))
    ]
    for load in loads[0] + loads[1]:
        load.start()
    barrier = pltpu.get_barrier_semaphore()
    for step in (1, 2, -1, -2):
        pl.semaphore_signal(barrier, inc=1, device_id=device(step), device_id_type=MESH)

    last = blocks * ROWS

    def document_start(position):
        first = position * 0
        start = jnp.int32(0)
        for d in range(lengths.shape[1]):
            first = jnp.where(start <= position, start, first)
            start = start + lengths[0, d]
        return first

    def keys_cross(block):
        edge = block * ROWS
        return (edge - document_start(edge) <= COVER) | (edge >= last)

    keys0, keys1 = keys_cross(me), keys_cross(me + 1)

    for load in loads[0]:
        load.wait()
    pl.semaphore_wait(barrier, 4)

    routes = (
        (right1, from_left1, 1),
        (left1, from_right1, -1),
        (right2, from_left2, 1),
        (left2, from_right2, -1),
    )

    def message(s, i):
        staged, landed, step = routes[i]
        slot = s % SLOTS
        return pltpu.make_async_remote_copy(
            staged.at[slot],
            landed.at[s],
            msg_send.at[slot, i],
            msg_recv.at[s, i],
            device_id=device(step),
            device_id_type=MESH,
        )

    def start(s, which):
        for i in which:
            message(s, i).start()

    def reuse(s, which):
        @pl.when(s >= SLOTS)
        def _():
            for i in which:
                message(s - SLOTS, i).wait_send()

    def send_blocks(s):
        slot = s % SLOTS
        columns = span(jnp.minimum(s, chunks - 1))
        keep = (s + 3 * LAG) % 4
        back = jnp.where(s >= LAG, s - LAG + TURN, spare)
        reuse(s, (0, 1))
        for a, (own_key, own_query) in enumerate(((k_all, q_all), (v_all, g_all))):
            more = from_left2[back, a].astype(jnp.float32)
            more = jnp.where(keys0, 0.0, more)
            head = (far_q1[keep, a, :HALF] + more).astype(jnp.bfloat16)
            tail = far_q1[keep, a, HALF:].astype(jnp.bfloat16)
            right1[slot, a, :HALF] = jnp.where(keys1, own_key[:HALF, columns], head)
            right1[slot, a, HALF:] = jnp.where(keys1, own_key[HALF:, columns], tail)
            more = from_right2[back, a].astype(jnp.float32)
            more = jnp.where(keys1, more, 0.0)
            head = far_k1[keep, a, :HALF].astype(jnp.bfloat16)
            tail = (far_k1[keep, a, HALF:] + more).astype(jnp.bfloat16)
            left1[slot, a, :HALF] = jnp.where(keys0, head, own_query[:HALF, columns])
            left1[slot, a, HALF:] = jnp.where(keys0, tail, own_query[HALF:, columns])
        start(s, (0, 1))

    def send_halves(s):
        slot = s % SLOTS
        done = (s + TURN) % 2
        reuse(s, (2, 3))
        for a in range(2):
            right2[slot, a] = jnp.where(keys1, from_left1[s, a, ROWS - HALF :], far_q2[done, a])
            left2[slot, a] = jnp.where(keys0, far_k2[done, a], from_right1[s, a, :HALF])
        start(s, (2, 3))

    stat_routes = (
        (to_right1, stats_left1, 1),
        (to_left1, stats_right1, -1),
        (to_right2, stats_left2, 2),
        (to_left2, stats_right2, -2),
    )

    def stat_message(c, i):
        staged, landed, step = stat_routes[i]
        return pltpu.make_async_remote_copy(
            staged.at[c],
            landed.at[c],
            stat_send.at[c, i],
            stat_recv.at[c, i],
            device_id=device(step),
            device_id_type=MESH,
        )

    def halves(log, along, first):
        part = slice(first, first + HALF)
        return jnp.concatenate([log[:, part], along[:, part]], axis=1)

    def unpack(row, fill):
        rest = jnp.full((1, ROWS - HALF), fill, jnp.float32)
        return (
            jnp.concatenate([row[:, :HALF], rest], axis=1),
            jnp.concatenate([row[:, HALF:], jnp.zeros_like(rest)], axis=1),
        )

    scale = DH ** (-0.5)
    pad = jnp.zeros((ROWS - HALF, DH), jnp.bfloat16)

    def met_keys(c, a, h):
        inner = slice(h * DH, (h + 1) * DH)
        own = (k_all, v_all)[a][:, pl.ds(pl.multiple_of(c * width + h * DH, DH), DH)]
        return jnp.concatenate(
            [from_left2[c, a, :, inner], from_left1[c, a, :, inner], own], axis=0
        )

    def met_queries(c, a, h):
        inner = slice(h * DH, (h + 1) * DH)
        own = (q_all, g_all)[a][:, pl.ds(pl.multiple_of(c * width + h * DH, DH), DH)]
        return jnp.concatenate(
            [own, from_right1[c, a, :, inner], from_right2[c, a, :, inner], pad], axis=0
        )

    def partial_totals(c):
        slot = c % (PATIENCE + 1)
        for h in range(HEADS):
            score = dot(met_keys(c, 0, h), met_queries(c, 0, h), NT) * (scale * LOG2E) + bias[...]
            pull = dot(met_keys(c, 1, h), met_queries(c, 1, h), NT)
            pulls[slot, h] = pull
            peak = jnp.max(score, axis=0, keepdims=True)
            power = jnp.exp2(score - peak)
            powers[slot, h] = power
            peaks[slot, pl.ds(h, 1), :] = peak
            total = jnp.sum(power, axis=0, keepdims=True)
            along = jnp.sum(power * pull, axis=0, keepdims=True) / total
            log = peak + jnp.log2(total)
            stats[slot, pl.ds(2 * h, 1), :] = log
            stats[slot, pl.ds(2 * h + 1, 1), :] = along
            for one, two, first, second in (
                (to_left1, to_left2, 0, ROWS),
                (to_right1, to_right2, ROWS, 2 * ROWS),
            ):
                one[c, pl.ds(3 * h, 1), :] = log[:, first : first + ROWS]
                one[c, pl.ds(3 * h + 1, 1), :] = along[:, first : first + ROWS]
                one[c, pl.ds(3 * h + 2, 1), :] = halves(log, along, second)
            to_left2[c, pl.ds(h, 1), :] = halves(log, along, 0)
            to_right2[c, pl.ds(h, 1), :] = halves(log, along, 2 * ROWS)
        for i in range(4):
            stat_message(c, i).start()

    def gradients(c):
        slot, done = c % (PATIENCE + 1), c % 2
        keep, turn = c % 8, c % 4
        for i in range(4):
            stat_message(c, i).wait()
        mine = stats[slot]
        left1, right1, left2, right2 = (
            landed[c] for landed in (stats_left1, stats_right1, stats_left2, stats_right2)
        )
        for h in range(HEADS):
            inner = slice(h * DH, (h + 1) * DH)
            near, far = 3 * h, slice(3 * h + 2, 3 * h + 3)
            left_log, left_along = unpack(left1[far], MASKED)
            right_log, right_along = unpack(right1[far], 0.0)
            left2_log, left2_along = unpack(left2[h : h + 1], MASKED)
            right2_log, right2_along = unpack(right2[h : h + 1], 0.0)
            logs = [
                mine[2 * h : 2 * h + 1],
                jnp.concatenate([left1[near : near + 1], left_log, right_log], axis=1),
                jnp.concatenate([left2_log, right1[near : near + 1], right2_log], axis=1),
            ]
            alongs = [
                mine[2 * h + 1 : 2 * h + 2],
                jnp.concatenate([left1[near + 1 : near + 2], left_along, right_along], axis=1),
                jnp.concatenate([left2_along, right1[near + 1 : near + 2], right2_along], axis=1),
            ]
            peak = jnp.maximum(jnp.maximum(logs[0], logs[1]), logs[2])
            shares = [jnp.exp2(log - peak) for log in logs]
            total = shares[0] + shares[1] + shares[2]
            log_total = peak + jnp.log2(total)
            along = sum(share * part for share, part in zip(shares, alongs)) / total
            lse_out[0, pl.ds(c * HEADS + h, 1), :] = log_total[:, :ROWS] * LN2
            weight = powers[slot, h] * jnp.exp2(peaks[slot, pl.ds(h, 1), :] - log_total)
            slope = (weight * (pulls[slot, h] - along)).astype(jnp.bfloat16)
            weight = weight.astype(jnp.bfloat16)
            keys, values = met_keys(c, 0, h), met_keys(c, 1, h)
            queries, grads = met_queries(c, 0, h), met_queries(c, 1, h)
            for a, (query_part, key_part) in enumerate(
                (
                    (dot(weight, values, TN), dot(slope, queries, NN) * scale),
                    (dot(slope, keys, TN) * scale, dot(weight, grads, NN)),
                )
            ):
                own_q[keep, a, :, inner] = query_part[:ROWS]
                far_q1[turn, a, :, inner] = query_part[ROWS : 2 * ROWS]
                far_q2[done, a, :, inner] = query_part[2 * ROWS : 2 * ROWS + HALF].astype(
                    jnp.bfloat16
                )
                own_k[keep, a, :, inner] = key_part[COVER:]
                far_k1[turn, a, :, inner] = key_part[HALF:COVER]
                far_k2[done, a, :, inner] = key_part[:HALF].astype(jnp.bfloat16)

    def finish(s):
        c = s - LAG
        keep = c % 8
        columns = span(c)
        for a, (query_out, key_out) in enumerate(((o_out, dk_out), (dq_out, dv_out))):
            query_part = jnp.where(keys0, 0.0, from_left1[s, a].astype(jnp.float32))
            query_out[0, :, columns] = (own_q[keep, a] + query_part).astype(jnp.bfloat16)
            key_part = jnp.where(keys1, from_right1[s, a].astype(jnp.float32), 0.0)
            key_out[0, :, columns] = (own_k[keep, a] + key_part).astype(jnp.bfloat16)

    for far in (far_q1, far_q2, far_k1, far_k2):
        far[...] = jnp.zeros(far.shape, far.dtype)
    for landed in (from_left2, from_right2):
        landed[spare] = jnp.zeros(landed.shape[1:], landed.dtype)
    for s in range(AHEAD):
        send_blocks(s)

    query_pos = me * ROWS + lax.broadcasted_iota(jnp.int32, (1, QUERIES), 1)
    first = document_start(query_pos)
    lane = lax.broadcasted_iota(jnp.int32, (1, QUERIES), 1)
    first = jnp.where((query_pos >= last) | (lane >= 2 * ROWS + HALF), NEVER, first)
    first = jnp.where((lane >= ROWS) & (lane * 0 + keys1.astype(jnp.int32) > 0), NEVER, first)
    key_pos = me * ROWS - COVER + lax.broadcasted_iota(jnp.int32, (KEYS, 1), 0)
    seen_pos = jnp.where(
        (key_pos < me * ROWS) & (key_pos * 0 + keys0.astype(jnp.int32) == 0), -1, key_pos
    )
    bias[...] = jnp.where((seen_pos >= first) & (key_pos <= query_pos), 0.0, MASKED)

    for load in loads[1]:
        load.wait()

    def one_step(s, carry):
        for i in (0, 1):
            message(s, i).wait_recv()

        @pl.when(s < chunks + TURN)
        def _():
            send_halves(s)

        @pl.when((s >= DEPTH) & (s < chunks + TURN + DEPTH))
        def _():
            for i in (2, 3):
                message(s - DEPTH, i).wait_recv()

        @pl.when((s >= DEPTH) & (s < chunks + DEPTH))
        def _():
            partial_totals(s - DEPTH)

        @pl.when(s + AHEAD < steps)
        def _():
            send_blocks(s + AHEAD)

        @pl.when((s >= DEPTH + PATIENCE) & (s < chunks + DEPTH + PATIENCE))
        def _():
            gradients(s - DEPTH - PATIENCE)

        @pl.when(s >= LAG)
        def _():
            finish(s)

        return carry

    lax.fori_loop(0, steps, one_step, 0)
    for which, count in (((0, 1), steps), ((2, 3), chunks + TURN)):
        for s in range(count - SLOTS, count):
            for i in which:
                message(s, i).wait_send()


def write_out(*refs):
    sems = refs[10]
    moves = [pltpu.make_async_copy(refs[i], refs[5 + i], sems.at[i]) for i in range(5)]
    for move in moves:
        move.start()
    for move in moves:
        move.wait()


def write_results(*results):
    return pl.pallas_call(
        write_out,
        name="write_out",
        out_shape=tuple(jax.ShapeDtypeStruct(r.shape, r.dtype) for r in results),
        in_specs=[pl.BlockSpec(memory_space=pltpu.VMEM)] * 5,
        out_specs=(pl.BlockSpec(memory_space=pl.ANY),) * 5,
        scratch_shapes=[pltpu.SemaphoreType.DMA((5,))],
        compiler_params=pltpu.CompilerParams(vmem_limit_bytes=2**20),
    )(*(pltpu.with_memory_space_constraint(r, pltpu.VMEM) for r in results))


def attend(queries, key_vectors, value_vectors, out_grad, lengths):
    _, rows, all_width = queries.shape
    heads = all_width // DH
    width = HEADS * DH
    chunks = heads // HEADS
    steps = chunks + LAG
    block = pltpu.VMEM(queries.shape, jnp.bfloat16)
    totals = pltpu.VMEM((1, heads, rows), jnp.float32)
    anywhere = pl.BlockSpec(memory_space=pl.ANY)
    low = functools.partial(pltpu.VMEM, dtype=jnp.bfloat16)
    wide = functools.partial(pltpu.VMEM, dtype=jnp.float32)
    copies = pltpu.SemaphoreType.DMA
    results = pl.pallas_call(
        kernel,
        name="chain_attention",
        out_shape=(block, totals, block, block, block),
        in_specs=[pl.BlockSpec(memory_space=pltpu.SMEM)] + [anywhere] * 4,
        out_specs=(pl.BlockSpec(memory_space=pltpu.VMEM),) * 5,
        scratch_shapes=[low((rows, all_width))] * 4
        + [low((SLOTS, 2, ROWS, width)), low((SLOTS, 2, HALF, width))] * 2
        + [low((steps, 2, ROWS, width)), low((chunks + TURN + 1, 2, HALF, width))] * 2
        + [wide((4, 2, ROWS, width)), low((2, 2, HALF, width))] * 2
        + [
            wide((8, 2, ROWS, width)),
            wide((8, 2, ROWS, width)),
            wide((PATIENCE + 1, HEADS, KEYS, QUERIES)),
            wide((PATIENCE + 1, HEADS, KEYS, QUERIES)),
            wide((PATIENCE + 1, HEADS, QUERIES)),
            wide((PATIENCE + 1, 2 * HEADS, QUERIES)),
        ]
        + [wide((chunks, 3 * HEADS, ROWS)), wide((chunks, HEADS, ROWS))] * 4
        + [
            wide((KEYS, QUERIES)),
            copies((2, 4)),
            copies((SLOTS, 4)),
            copies((steps, 4)),
            copies((chunks, 4)),
            copies((chunks, 4)),
        ],
        compiler_params=pltpu.CompilerParams(
            collective_id=0, has_side_effects=True, vmem_limit_bytes=48 * 2**20
        ),
    )(lengths, queries, key_vectors, value_vectors, out_grad)
    return write_results(*results)


def solution(mesh):
    block = P("dp", "ctx", None)
    in_specs = (block, block, block, block, P("dp", None))
    out_specs = (block, P("dp", None, "ctx"), block, block, block)
    return jax.shard_map(attend, mesh=mesh, in_specs=in_specs, out_specs=out_specs, check_vma=False)
```

```python
import functools

import jax
import jax.numpy as jnp
from jax import lax
from jax.experimental import pallas as pl
from jax.experimental.pallas import tpu as pltpu
from jax.sharding import PartitionSpec as P

DH = 128
ROWS = 128
HALF = 64
LONGEST = 384
COVER = LONGEST // 2
KEYS = COVER + ROWS
QUERIES = 3 * ROWS
HEADS = 2
AHEAD = 2
DEPTH = 1
PATIENCE = 1
TURN = DEPTH + PATIENCE + 1
LAG = TURN + DEPTH + AHEAD
SLOTS = AHEAD + 1
TOGETHER = 1
LOG2E = 1.4426950408889634
LN2 = 0.6931471805599453
MASKED = -1e30
NEVER = 1 << 30
MESH = pl.DeviceIdType.MESH

NT = (((1,), (1,)), ((), ()))
NN = (((1,), (0,)), ((), ()))
TN = (((0,), (0,)), ((), ()))


def dot(a, b, dims):
    return lax.dot_general(a, b, dims, preferred_element_type=jnp.float32)


def kernel(
    lengths,
    q_in,
    k_in,
    v_in,
    g_in,
    o_out,
    lse_out,
    dq_out,
    dk_out,
    dv_out,
    q_all,
    k_all,
    v_all,
    g_all,
    right1,
    right2,
    left1,
    left2,
    from_left1,
    from_left2,
    from_right1,
    from_right2,
    far_q1,
    far_q2,
    far_k1,
    far_k2,
    own_q,
    own_k,
    powers,
    pulls,
    peaks,
    stats,
    to_left1,
    to_left2,
    to_right1,
    to_right2,
    stats_left1,
    stats_left2,
    stats_right1,
    stats_right2,
    bias,
    in_local,
    msg_send,
    msg_recv,
    stat_send,
    stat_recv,
    pair,
):
    width = HEADS * DH
    chunks = q_all.shape[1] // width
    steps = chunks + LAG
    spare = chunks + TURN
    blocks = lax.axis_size("ctx")
    dp = lax.axis_index("dp")
    me = lax.axis_index("ctx")

    def device(step):
        return (dp, (me + step + blocks) % blocks)

    def span(c):
        return pl.ds(pl.multiple_of(c * width, width), width)

    early = 8 * DH
    loads = [
        [
            pltpu.make_async_copy(source.at[0, :, part], kept.at[:, part], in_local.at[p, i])
            for i, (source, kept) in enumerate(
                ((k_in, k_all), (v_in, v_all), (q_in, q_all), (g_in, g_all))
            )
        ]
        for p, part in enumerate((slice(0, early), slice(early, q_all.shape[1])))
    ]
    for load in loads[0] + loads[1]:
        load.start()
    barrier = pltpu.get_barrier_semaphore()
    for step in (1, 2, -1, -2):
        pl.semaphore_signal(barrier, inc=1, device_id=device(step), device_id_type=MESH)
    partner = (dp + 1 - 2 * (dp % 2), me)
    pl.semaphore_signal(barrier, inc=1, device_id=partner, device_id_type=MESH)

    last = blocks * ROWS

    def document_start(position):
        first = position * 0
        start = jnp.int32(0)
        for d in range(lengths.shape[1]):
            first = jnp.where(start <= position, start, first)
            start = start + lengths[0, d]
        return first

    def keys_cross(block):
        edge = block * ROWS
        return (edge - document_start(edge) <= COVER) | (edge >= last)

    keys0, keys1 = keys_cross(me), keys_cross(me + 1)

    for load in loads[0]:
        load.wait()
    pl.semaphore_wait(barrier, 5)

    routes = (
        (right1, from_left1, 1),
        (left1, from_right1, -1),
        (right2, from_left2, 1),
        (left2, from_right2, -1),
    )

    def message(s, i):
        staged, landed, step = routes[i]
        slot = s % SLOTS
        return pltpu.make_async_remote_copy(
            staged.at[slot],
            landed.at[s],
            msg_send.at[slot, i],
            msg_recv.at[s, i],
            device_id=device(step),
            device_id_type=MESH,
        )

    def start(s, which):
        for i in which:
            message(s, i).start()

    def reuse(s, which):
        @pl.when(s >= SLOTS)
        def _():
            for i in which:
                message(s - SLOTS, i).wait_send()

    def send_blocks(s):
        slot = s % SLOTS
        columns = span(jnp.minimum(s, chunks - 1))
        keep = (s + 3 * LAG) % 4
        back = jnp.where(s >= LAG, s - LAG + TURN, spare)
        reuse(s, (0, 1))
        for a, (own_key, own_query) in enumerate(((k_all, q_all), (v_all, g_all))):
            more = from_left2[back, a].astype(jnp.float32)
            more = jnp.where(keys0, 0.0, more)
            head = (far_q1[keep, a, :HALF] + more).astype(jnp.bfloat16)
            tail = far_q1[keep, a, HALF:].astype(jnp.bfloat16)
            right1[slot, a, :HALF] = jnp.where(keys1, own_key[:HALF, columns], head)
            right1[slot, a, HALF:] = jnp.where(keys1, own_key[HALF:, columns], tail)
            more = from_right2[back, a].astype(jnp.float32)
            more = jnp.where(keys1, more, 0.0)
            head = far_k1[keep, a, :HALF].astype(jnp.bfloat16)
            tail = (far_k1[keep, a, HALF:] + more).astype(jnp.bfloat16)
            left1[slot, a, :HALF] = jnp.where(keys0, head, own_query[:HALF, columns])
            left1[slot, a, HALF:] = jnp.where(keys0, tail, own_query[HALF:, columns])
        start(s, (0, 1))

    def send_halves(s):
        slot = s % SLOTS
        done = (s + TURN) % 2
        reuse(s, (2, 3))
        for a in range(2):
            right2[slot, a] = jnp.where(keys1, from_left1[s, a, ROWS - HALF :], far_q2[done, a])
            left2[slot, a] = jnp.where(keys0, far_k2[done, a], from_right1[s, a, :HALF])
        start(s, (2, 3))

    stat_routes = (
        (to_right1, stats_left1, 1),
        (to_left1, stats_right1, -1),
        (to_right2, stats_left2, 2),
        (to_left2, stats_right2, -2),
    )

    def stat_message(c, i):
        staged, landed, step = stat_routes[i]
        return pltpu.make_async_remote_copy(
            staged.at[c],
            landed.at[c],
            stat_send.at[c, i],
            stat_recv.at[c, i],
            device_id=device(step),
            device_id_type=MESH,
        )

    def halves(log, along, first):
        part = slice(first, first + HALF)
        return jnp.concatenate([log[:, part], along[:, part]], axis=1)

    def unpack(row, fill):
        rest = jnp.full((1, ROWS - HALF), fill, jnp.float32)
        return (
            jnp.concatenate([row[:, :HALF], rest], axis=1),
            jnp.concatenate([row[:, HALF:], jnp.zeros_like(rest)], axis=1),
        )

    scale = DH ** (-0.5)
    pad = jnp.zeros((ROWS - HALF, DH), jnp.bfloat16)

    def met_keys(c, a, h):
        inner = slice(h * DH, (h + 1) * DH)
        own = (k_all, v_all)[a][:, pl.ds(pl.multiple_of(c * width + h * DH, DH), DH)]
        return jnp.concatenate(
            [from_left2[c, a, :, inner], from_left1[c, a, :, inner], own], axis=0
        )

    def met_queries(c, a, h):
        inner = slice(h * DH, (h + 1) * DH)
        own = (q_all, g_all)[a][:, pl.ds(pl.multiple_of(c * width + h * DH, DH), DH)]
        return jnp.concatenate(
            [own, from_right1[c, a, :, inner], from_right2[c, a, :, inner], pad], axis=0
        )

    def partial_totals(c):
        slot = c % (PATIENCE + 1)
        for h in range(HEADS):
            score = dot(met_keys(c, 0, h), met_queries(c, 0, h), NT) * (scale * LOG2E) + bias[...]
            pull = dot(met_keys(c, 1, h), met_queries(c, 1, h), NT)
            pulls[slot, h] = pull
            peak = jnp.max(score, axis=0, keepdims=True)
            power = jnp.exp2(score - peak)
            powers[slot, h] = power
            peaks[slot, pl.ds(h, 1), :] = peak
            total = jnp.sum(power, axis=0, keepdims=True)
            along = jnp.sum(power * pull, axis=0, keepdims=True) / total
            log = peak + jnp.log2(total)
            stats[slot, pl.ds(2 * h, 1), :] = log
            stats[slot, pl.ds(2 * h + 1, 1), :] = along
            for one, two, first, second in (
                (to_left1, to_left2, 0, ROWS),
                (to_right1, to_right2, ROWS, 2 * ROWS),
            ):
                one[c, pl.ds(3 * h, 1), :] = log[:, first : first + ROWS]
                one[c, pl.ds(3 * h + 1, 1), :] = along[:, first : first + ROWS]
                one[c, pl.ds(3 * h + 2, 1), :] = halves(log, along, second)
            to_left2[c, pl.ds(h, 1), :] = halves(log, along, 0)
            to_right2[c, pl.ds(h, 1), :] = halves(log, along, 2 * ROWS)
        for i in range(4):
            stat_message(c, i).start()

    def gradients(c):
        slot, done = c % (PATIENCE + 1), c % 2
        keep, turn = c % 8, c % 4
        for i in range(4):
            stat_message(c, i).wait()
        mine = stats[slot]
        left1, right1, left2, right2 = (
            landed[c] for landed in (stats_left1, stats_right1, stats_left2, stats_right2)
        )
        for h in range(HEADS):
            inner = slice(h * DH, (h + 1) * DH)
            near, far = 3 * h, slice(3 * h + 2, 3 * h + 3)
            left_log, left_along = unpack(left1[far], MASKED)
            right_log, right_along = unpack(right1[far], 0.0)
            left2_log, left2_along = unpack(left2[h : h + 1], MASKED)
            right2_log, right2_along = unpack(right2[h : h + 1], 0.0)
            logs = [
                mine[2 * h : 2 * h + 1],
                jnp.concatenate([left1[near : near + 1], left_log, right_log], axis=1),
                jnp.concatenate([left2_log, right1[near : near + 1], right2_log], axis=1),
            ]
            alongs = [
                mine[2 * h + 1 : 2 * h + 2],
                jnp.concatenate([left1[near + 1 : near + 2], left_along, right_along], axis=1),
                jnp.concatenate([left2_along, right1[near + 1 : near + 2], right2_along], axis=1),
            ]
            peak = jnp.maximum(jnp.maximum(logs[0], logs[1]), logs[2])
            shares = [jnp.exp2(log - peak) for log in logs]
            total = shares[0] + shares[1] + shares[2]
            log_total = peak + jnp.log2(total)
            along = sum(share * part for share, part in zip(shares, alongs)) / total
            lse_out[0, pl.ds(c * HEADS + h, 1), :] = log_total[:, :ROWS] * LN2
            weight = powers[slot, h] * jnp.exp2(peaks[slot, pl.ds(h, 1), :] - log_total)
            slope = (weight * (pulls[slot, h] - along)).astype(jnp.bfloat16)
            weight = weight.astype(jnp.bfloat16)
            keys, values = met_keys(c, 0, h), met_keys(c, 1, h)
            queries, grads = met_queries(c, 0, h), met_queries(c, 1, h)
            for a, (query_part, key_part) in enumerate(
                (
                    (dot(weight, values, TN), dot(slope, queries, NN) * scale),
                    (dot(slope, keys, TN) * scale, dot(weight, grads, NN)),
                )
            ):
                own_q[keep, a, :, inner] = query_part[:ROWS]
                far_q1[turn, a, :, inner] = query_part[ROWS : 2 * ROWS]
                far_q2[done, a, :, inner] = query_part[2 * ROWS : 2 * ROWS + HALF].astype(
                    jnp.bfloat16
                )
                own_k[keep, a, :, inner] = key_part[COVER:]
                far_k1[turn, a, :, inner] = key_part[HALF:COVER]
                far_k2[done, a, :, inner] = key_part[:HALF].astype(jnp.bfloat16)

    def finish(s):
        c = s - LAG
        keep = c % 8
        columns = span(c)
        for a, (query_out, key_out) in enumerate(((o_out, dk_out), (dq_out, dv_out))):
            query_part = jnp.where(keys0, 0.0, from_left1[s, a].astype(jnp.float32))
            query_out[0, :, columns] = (own_q[keep, a] + query_part).astype(jnp.bfloat16)
            key_part = jnp.where(keys1, from_right1[s, a].astype(jnp.float32), 0.0)
            key_out[0, :, columns] = (own_k[keep, a] + key_part).astype(jnp.bfloat16)

    for far in (far_q1, far_q2, far_k1, far_k2):
        far[...] = jnp.zeros(far.shape, far.dtype)
    for landed in (from_left2, from_right2):
        landed[spare] = jnp.zeros(landed.shape[1:], landed.dtype)
    for s in range(AHEAD):
        send_blocks(s)

    query_pos = me * ROWS + lax.broadcasted_iota(jnp.int32, (1, QUERIES), 1)
    first = document_start(query_pos)
    lane = lax.broadcasted_iota(jnp.int32, (1, QUERIES), 1)
    first = jnp.where((query_pos >= last) | (lane >= 2 * ROWS + HALF), NEVER, first)
    first = jnp.where((lane >= ROWS) & (lane * 0 + keys1.astype(jnp.int32) > 0), NEVER, first)
    key_pos = me * ROWS - COVER + lax.broadcasted_iota(jnp.int32, (KEYS, 1), 0)
    seen_pos = jnp.where(
        (key_pos < me * ROWS) & (key_pos * 0 + keys0.astype(jnp.int32) == 0), -1, key_pos
    )
    bias[...] = jnp.where((seen_pos >= first) & (key_pos <= query_pos), 0.0, MASKED)

    for load in loads[1]:
        load.wait()

    def one_step(s, carry):
        pl.semaphore_signal(pair, inc=1, device_id=partner, device_id_type=MESH)

        @pl.when(s >= TOGETHER)
        def _():
            pl.semaphore_wait(pair, 1)

        for i in (0, 1):
            message(s, i).wait_recv()

        @pl.when(s < chunks + TURN)
        def _():
            send_halves(s)

        @pl.when((s >= DEPTH) & (s < chunks + TURN + DEPTH))
        def _():
            for i in (2, 3):
                message(s - DEPTH, i).wait_recv()

        @pl.when((s >= DEPTH) & (s < chunks + DEPTH))
        def _():
            partial_totals(s - DEPTH)

        @pl.when(s + AHEAD < steps)
        def _():
            send_blocks(s + AHEAD)

        @pl.when((s >= DEPTH + PATIENCE) & (s < chunks + DEPTH + PATIENCE))
        def _():
            gradients(s - DEPTH - PATIENCE)

        @pl.when(s >= LAG)
        def _():
            finish(s)

        return carry

    lax.fori_loop(0, steps, one_step, 0)
    pl.semaphore_wait(pair, TOGETHER)
    for which, count in (((0, 1), steps), ((2, 3), chunks + TURN)):
        for s in range(count - SLOTS, count):
            for i in which:
                message(s, i).wait_send()


def write_out(*refs):
    sems = refs[10]
    moves = [pltpu.make_async_copy(refs[i], refs[5 + i], sems.at[i]) for i in range(5)]
    for move in moves:
        move.start()
    for move in moves:
        move.wait()


def write_results(*results):
    return pl.pallas_call(
        write_out,
        name="write_out",
        out_shape=tuple(jax.ShapeDtypeStruct(r.shape, r.dtype) for r in results),
        in_specs=[pl.BlockSpec(memory_space=pltpu.VMEM)] * 5,
        out_specs=(pl.BlockSpec(memory_space=pl.ANY),) * 5,
        scratch_shapes=[pltpu.SemaphoreType.DMA((5,))],
        compiler_params=pltpu.CompilerParams(vmem_limit_bytes=2**20),
    )(*(pltpu.with_memory_space_constraint(r, pltpu.VMEM) for r in results))


def attend(queries, key_vectors, value_vectors, out_grad, lengths):
    _, rows, all_width = queries.shape
    heads = all_width // DH
    width = HEADS * DH
    chunks = heads // HEADS
    steps = chunks + LAG
    block = pltpu.VMEM(queries.shape, jnp.bfloat16)
    totals = pltpu.VMEM((1, heads, rows), jnp.float32)
    anywhere = pl.BlockSpec(memory_space=pl.ANY)
    low = functools.partial(pltpu.VMEM, dtype=jnp.bfloat16)
    wide = functools.partial(pltpu.VMEM, dtype=jnp.float32)
    copies = pltpu.SemaphoreType.DMA
    results = pl.pallas_call(
        kernel,
        name="chain_attention",
        out_shape=(block, totals, block, block, block),
        in_specs=[pl.BlockSpec(memory_space=pltpu.SMEM)] + [anywhere] * 4,
        out_specs=(pl.BlockSpec(memory_space=pltpu.VMEM),) * 5,
        scratch_shapes=[low((rows, all_width))] * 4
        + [low((SLOTS, 2, ROWS, width)), low((SLOTS, 2, HALF, width))] * 2
        + [low((steps, 2, ROWS, width)), low((chunks + TURN + 1, 2, HALF, width))] * 2
        + [wide((4, 2, ROWS, width)), low((2, 2, HALF, width))] * 2
        + [
            wide((8, 2, ROWS, width)),
            wide((8, 2, ROWS, width)),
            wide((PATIENCE + 1, HEADS, KEYS, QUERIES)),
            wide((PATIENCE + 1, HEADS, KEYS, QUERIES)),
            wide((PATIENCE + 1, HEADS, QUERIES)),
            wide((PATIENCE + 1, 2 * HEADS, QUERIES)),
        ]
        + [wide((chunks, 3 * HEADS, ROWS)), wide((chunks, HEADS, ROWS))] * 4
        + [
            wide((KEYS, QUERIES)),
            copies((2, 4)),
            copies((SLOTS, 4)),
            copies((steps, 4)),
            copies((chunks, 4)),
            copies((chunks, 4)),
            pltpu.SemaphoreType.REGULAR,
        ],
        compiler_params=pltpu.CompilerParams(
            collective_id=0, has_side_effects=True, vmem_limit_bytes=48 * 2**20
        ),
    )(lengths, queries, key_vectors, value_vectors, out_grad)
    return write_results(*results)


def solution(mesh):
    block = P("dp", "ctx", None)
    in_specs = (block, block, block, block, P("dp", None))
    out_specs = (block, P("dp", None, "ctx"), block, block, block)
    return jax.shard_map(attend, mesh=mesh, in_specs=in_specs, out_specs=out_specs, check_vma=False)
```
